32 devices in a mesh: parts: 2 (over x), ep: 16 (over z, y, core).
Axes of the slice: x: 2, y: 2, z: 4, core: 2. Of those that a mesh axis runs over, the one named last changes fastest.
Arguments:
- queries: bfloat16 [1024, 8192], P(('parts', 'ep')), parts along dimension 0, may hold values from -128 to 128
- fresh_token_keys: bfloat16 [1024, 512], P(('parts', 'ep')), parts along dimension 0, may hold values from -4 to 4
- fresh_token_values: bfloat16 [1024, 512], P(('parts', 'ep')), parts along dimension 0, may hold values from -6 to 6
- pooled_keys: bfloat16 [8192, 16, 512], P(('parts', 'ep')), parts along dimension 0, may hold values from -6 to 6
- pooled_values: bfloat16 [8192, 16, 512], P(('parts', 'ep')), parts along dimension 0, may hold values from -6 to 6
- lengths: int32 [32, 32], P(('parts', 'ep')), parts along dimension 0, may hold values from 1 to 256, 3584 in all within a row
- page_order: int32 [32, 256], P(('parts', 'ep')), parts along dimension 0, may hold values from 0 to 255, each once within a row
- hidden: bfloat16 [1024, 4096], P(('parts', 'ep')), parts along dimension 0, may hold values from -40 to 40
- out_weight: bfloat16 [8192, 4096], P('ep'), may hold values from -1.25 to 1.25
- norm_gain: float32 [4096], replicated, may hold values from 0.25 to 1.75
- expert_ids: int32 [1024, 8], P(('parts', 'ep')), parts along dimension 0, may hold values from 0 to 15, all different within a row; in each aligned block of 32 rows (0 to 31, 32 to 63, ...) at most 16 rows name the same one
- gate_weights: float32 [1024, 8], P(('parts', 'ep')), parts along dimension 0, may hold values from 0.05 to 0.5
- expert_gate_up: bfloat16 [16, 4096, 1536], P('ep'), may hold values from -0.09375 to 0.09375
- expert_down: bfloat16 [16, 768, 4096], P('ep'), may hold values from -0.21875 to 0.21875
- mig_pages: int32 [32, 16], P(('parts', 'ep')), parts along dimension 0, may hold values from 0 to 255
- mig_dest: int32 [512, 1], P(('parts', 'ep')), parts along dimension 0, may hold values from 0 to 15; in each aligned block of 16 rows (0 to 15, 16 to 31, ...) no two rows name the same one
Outputs:
- layer_out: bfloat16 [1024, 4096], P(('parts', 'ep')), parts along dimension 0
- arrived_keys: bfloat16 [512, 16, 512], P(('parts', 'ep')), parts along dimension 0
- arrived_values: bfloat16 [512, 16, 512], P(('parts', 'ep')), parts along dimension 0
The draws below stay inside these ranges and needn't reach their ends.
There are 2 independent parts, one for each index of `parts`. The reference program is written for one: setup_inputs(seed, part) draws one part's arguments, and reference() takes and returns one part's arrays. A program takes and returns all parts, laid end to end along the dimension named above; an argument that names none is the same for every part. Nothing has to cross between parts.
Inputs may be any that keep to these rules, and one draw needn't show every extreme that they name: `lengths`: the 32 sequences of one device hold (224) * 16 cached tokens together. `page_order`: each row is a permutation of the device's pool pages. `expert_ids`: each row names 8 different experts; among the rows of one device no expert is named more than 16 times. `mig_dest`: among the rows of one device no destination is named twice.
All inputs are finite; a program needn't handle non-finite values.
Results may differ from the reference program's by a relative error of at most 0.0075.
Values may be sent and summed in bfloat16 or wider, within the bound.
A program may use at most 128 MiB of HBM per device.

```python
import math
import jax
import jax.numpy as jnp
import numpy as np
from jax import lax

D = 4096
QUERY_HEADS = 64
KEY_VALUE_HEADS = 4
HEAD_SIZE = 128
FFW = 768
TOPK = 8
PAGE_TOKENS = 16
MOST_SEQ_PAGES = 16
MIG_DEV = 16
SEQ_DEV = 32
INSTANCE_SEQS = 512
EXPERTS = 16
CAP = 16
DEVICE_POOL_PAGES = 256
N_EP = 16


def shared_keys(key):
    base_offset = jax.random.normal(jax.random.fold_in(key, 77), (INSTANCE_SEQS, KEY_VALUE_HEADS * HEAD_SIZE), jnp.float32)
    return jnp.clip(base_offset, -4.0, 4.0)


def draw_fresh_token_keys(key, part):
    base_offset = shared_keys(key)
    return base_offset.astype(jnp.bfloat16)


def draw_queries(key, part):
    key = jax.random.fold_in(key, 2)
    value_rows = jnp.clip(jax.random.normal(key, (INSTANCE_SEQS, QUERY_HEADS * HEAD_SIZE), jnp.float32), -4.0, 4.0)
    return value_rows.astype(jnp.bfloat16)


def draw_pooled_keys(key, part):
    key = jax.random.fold_in(key, 5)
    page_table = N_EP * DEVICE_POOL_PAGES
    value_rows = jnp.clip(jax.random.normal(key, (page_table, PAGE_TOKENS, KEY_VALUE_HEADS * HEAD_SIZE), jnp.float32), -6.0, 6.0)
    return value_rows.astype(jnp.bfloat16)


def draw_hidden(key, part):
    key = jax.random.fold_in(key, 4)
    noise = jnp.clip(jax.random.normal(jax.random.fold_in(key, 1), (INSTANCE_SEQS, D), jnp.float32), -5.0, 5.0)
    row_scale = jnp.exp(math.log(10.0) * jax.random.uniform(jax.random.fold_in(key, 2), (INSTANCE_SEQS, 1), jnp.float32))
    col_scale = jnp.exp(math.log(10.0) * jax.random.uniform(jax.random.fold_in(key, 3), (1, D), jnp.float32))
    value_rows = noise * row_scale * col_scale / 30.0
    return value_rows.astype(jnp.bfloat16)


def set_ends(entries, stream_key, low, high):
    place = [jax.random.randint(jax.random.fold_in(stream_key, axis), (), 0, length) for axis, length in enumerate(entries.shape)]
    longest = entries.shape.index(max(entries.shape))
    neighbour = place[:longest] + [(place[longest] + 1) % entries.shape[longest]] + place[longest + 1:]
    return entries.at[tuple(place)].set(low).at[tuple(neighbour)].set(high)


def steps_of(key, dims, shards, low, high):
    def one(dim, blocks):
        draws = jax.random.uniform(jax.random.fold_in(jax.random.fold_in(key, 6), dim), (blocks,), jnp.float32, low / len(shards), high / len(shards))
        return jnp.repeat(jnp.exp(draws), dims[dim] // blocks).reshape((-1,) + (1,) * (len(dims) - dim - 1))

    factor_of = one(*shards[0])
    for cut in shards[1:]:
        factor_of = factor_of * one(*cut)
    return factor_of


def length_profile(amount, total, most, skew):
    portions = [(1 << 20) // math.isqrt(standing ** skew) + 1 for standing in range(2, amount + 1)]
    rest, given = total - most - (amount - 1), [1] * (amount - 1)
    while rest > 0:
        candidates = [i for i in range(amount - 1) if given[i] < most]
        whole, remaining = sum([portions[i] for i in candidates]), rest
        for i in candidates:
            addition = min(most - given[i], max(1, remaining * portions[i] // whole), rest)
            given[i] = given[i] + addition
            rest = rest - addition
    return np.array([most] + given)


def uneven_parts(rng, amount, total, reach, slope):
    if amount == 2:
        one = jax.random.randint(rng, (), max(1, total - reach), min(reach, total - 1) + 1)
        return jnp.stack([one, total - one])
    tallies = jnp.asarray(length_profile(amount, total, reach, slope), jnp.int32)
    pairs = (amount - 1) // 2
    giver, sink = tallies[1:1 + 2 * pairs:2], tallies[2:2 + 2 * pairs:2]
    room = jnp.minimum(giver - 1, reach - sink)
    shifted = jax.random.randint(jax.random.fold_in(rng, 1), (pairs,), 0, 1 << 20) % (room + 1)
    tallies = tallies.at[1:1 + 2 * pairs:2].set(giver - shifted).at[2:2 + 2 * pairs:2].set(sink + shifted)
    return tallies[jax.random.permutation(jax.random.fold_in(rng, 2), amount)]


def deal_out(rng, own, number, rows, amount, top, reach, skew):
    ranking = jax.random.permutation(rng, amount)
    packed, usual = load_shares(amount, rows * top, reach, skew, True), load_shares(amount, rows * top, reach, skew, False)
    places = jnp.arange(amount)

    def named(tallies, turn):
        used = int((tallies > 0).sum())
        fixed = max(1, used // 4)
        shifted = fixed + (places - fixed + turn * (used - fixed)) % max(1, amount - fixed)
        return jnp.zeros((amount,), jnp.int32).at[ranking[jnp.where(places < fixed, places, shifted)]].set(jnp.asarray(tallies, jnp.int32))

    tallies = jnp.where(number % 4 == 0, named(packed, number // 4), named(usual, number - number // 4 - 1))
    mixed = jax.random.permutation(jax.random.fold_in(own, 3), amount)
    donor, sink = mixed[0:amount // 2 * 2:2], mixed[1:amount // 2 * 2:2]
    margin = jnp.minimum(tallies[donor] - 1, reach - tallies[sink]) // 2
    margin = jnp.where((donor == ranking[0]) | (sink == ranking[0]) | (tallies[sink] == 0), 0, jnp.maximum(margin, 0))
    shifted = jax.random.randint(jax.random.fold_in(own, 4), (amount // 2,), 0, 1 << 20) % (margin + 1)
    tallies = tallies.at[donor].add(-shifted).at[sink].add(shifted)
    members = jnp.searchsorted(jnp.cumsum(tallies), jnp.arange(rows * top), side="right").astype(jnp.int32)
    table = members.reshape(top, rows).T
    table = table[jax.random.permutation(jax.random.fold_in(own, 1), rows)]
    turn = jax.random.randint(jax.random.fold_in(own, 2), (rows, 1), 0, top)
    return jnp.take_along_axis(table, (jnp.arange(top)[None, :] + turn) % top, axis=1)


def load_shares(number_of, total, most, lean, full):
    loads = [(1 << 20) // math.isqrt(standing ** lean) + 1 for standing in range(1, number_of + 1)]
    largest = most if full else min(most, max(-(-total // number_of), total * loads[0] // sum(loads)))
    least = 1 if total - largest >= number_of - 1 else 0
    given, spare = [largest] + [least] * (number_of - 1), total - largest - least * (number_of - 1)
    while spare > 0:
        movable = [i for i in range(1, number_of) if given[i] < largest] or [i for i in range(1, number_of) if given[i] < most]
        whole, budget = sum([loads[i] for i in movable]), spare
        for i in movable:
            addition = min(most - given[i], max(1, budget * loads[i] // whole), spare)
            given[i] = given[i] + addition
            spare = spare - addition
    return np.array(given)


def centred(key, dims, spread, limit, cuts=(), held_as=jnp.bfloat16):
    values = jax.random.normal(key, dims, jnp.float32) * spread
    if len(cuts) > 0:
        values = steps_of(key, dims, cuts, -0.22, 0.18) * values
    return jnp.clip(values, min=-limit, max=limit).astype(held_as)


def setup_inputs(seed: int = 0, part: int = 0) -> dict:
    arg_keys = jax.random.split(jax.random.key(seed), 17)
    part_splits = jax.random.split(jax.random.fold_in(arg_keys[16], part), 17)
    queries = draw_queries(jax.random.fold_in(jax.random.fold_in(arg_keys[16], part), 71), part)
    fresh_token_keys = draw_fresh_token_keys(jax.random.fold_in(jax.random.fold_in(arg_keys[16], part), 71), part)
    fresh_token_values = centred(part_splits[2], (INSTANCE_SEQS, KEY_VALUE_HEADS * HEAD_SIZE), 1.0, 6.0, ((0, 16),))
    pooled_keys = draw_pooled_keys(jax.random.fold_in(jax.random.fold_in(arg_keys[16], part), 71), part)
    pooled_values = centred(part_splits[4], (N_EP * DEVICE_POOL_PAGES, PAGE_TOKENS, KEY_VALUE_HEADS * HEAD_SIZE), 1.0, 6.0, ((0, 16),))
    lengths = jax.vmap(lambda own: uneven_parts(own, SEQ_DEV, (DEVICE_POOL_PAGES - SEQ_DEV) * PAGE_TOKENS, MOST_SEQ_PAGES * PAGE_TOKENS, 2))(jax.random.split(part_splits[5], N_EP)).reshape((N_EP, SEQ_DEV)).astype(jnp.int32)
    page_order = jax.vmap(lambda own: jax.random.permutation(own, DEVICE_POOL_PAGES))(jax.random.split(part_splits[6], N_EP)).reshape((N_EP, DEVICE_POOL_PAGES)).astype(jnp.int32)
    hidden = draw_hidden(jax.random.fold_in(jax.random.fold_in(arg_keys[16], part), 71), part)
    out_weight = centred(arg_keys[8], (QUERY_HEADS * HEAD_SIZE, D), (8.0 / (QUERY_HEADS * HEAD_SIZE) ** 0.5), 1.25, ((0, 16),))
    norm_gain = jnp.clip(1.0 + 0.15 * jax.random.normal(arg_keys[9], (D,), jnp.float32), 0.25, 1.75)
    expert_ids_keys = jax.random.split(jax.random.fold_in(part_splits[10], 1), INSTANCE_SEQS // SEQ_DEV)
    expert_ids_turns = jax.random.permutation(jax.random.fold_in(part_splits[10], 3), INSTANCE_SEQS // SEQ_DEV)
    expert_ids = jax.vmap(lambda own, number: deal_out(jax.random.fold_in(part_splits[10], 2), own, number, SEQ_DEV, EXPERTS, TOPK, CAP, 2))(expert_ids_keys, expert_ids_turns).reshape((INSTANCE_SEQS, TOPK))
    gate_weights = jnp.clip(jnp.exp(math.log(0.5) - 2.3025851 * jax.random.uniform(part_splits[11], (INSTANCE_SEQS, TOPK), jnp.float32) ** steps_of(part_splits[11], (INSTANCE_SEQS, TOPK), ((0, 16),), -0.2, 0.2)), 0.05, 0.5)
    expert_gate_up = centred(arg_keys[12], (EXPERTS, D, 2 * FFW), D ** -0.5, 0.09375, ((0, 16),))
    expert_down = centred(arg_keys[13], (EXPERTS, FFW, D), FFW ** -0.5, 0.21875, ((0, 16),))
    mig_pages = set_ends(jax.random.randint(part_splits[14], (N_EP, MIG_DEV), 0, DEVICE_POOL_PAGES), jax.random.fold_in(part_splits[14], 1), 0, DEVICE_POOL_PAGES - 1).astype(jnp.int32)
    mig_dest_keys = jax.random.split(jax.random.fold_in(part_splits[15], 1), (N_EP * MIG_DEV) // MIG_DEV)
    mig_dest_turns = jax.random.permutation(jax.random.fold_in(part_splits[15], 3), (N_EP * MIG_DEV) // MIG_DEV)
    mig_dest = jax.vmap(lambda own, number: deal_out(jax.random.fold_in(part_splits[15], 2), own, number, MIG_DEV, N_EP, 1, 1, 1))(mig_dest_keys, mig_dest_turns).reshape((N_EP * MIG_DEV, 1))
    return dict(queries=queries, fresh_token_keys=fresh_token_keys, fresh_token_values=fresh_token_values, pooled_keys=pooled_keys, pooled_values=pooled_values, lengths=lengths, page_order=page_order, hidden=hidden, out_weight=out_weight, norm_gain=norm_gain, expert_ids=expert_ids, gate_weights=gate_weights, expert_gate_up=expert_gate_up, expert_down=expert_down, mig_pages=mig_pages, mig_dest=mig_dest)


def attend_device(queries, fresh_token_keys, fresh_token_values, pooled_keys, pooled_values, lengths, page_order):
    sequence_count = queries.shape[0]
    pages_dev = page_order.shape[0]
    counts = (lengths + (PAGE_TOKENS - 1)) // PAGE_TOKENS
    starts = (jnp.cumsum(counts) - counts).astype(jnp.int32)
    logical = starts[:, None] + jnp.arange(MOST_SEQ_PAGES, dtype=jnp.int32)[None, :]
    physical_page = page_order[jnp.clip(logical, 0, pages_dev - 1)]
    every_key = pooled_keys[physical_page].reshape(sequence_count, MOST_SEQ_PAGES * PAGE_TOKENS, KEY_VALUE_HEADS, HEAD_SIZE).astype(jnp.float32)
    every_value = pooled_values[physical_page].reshape(sequence_count, MOST_SEQ_PAGES * PAGE_TOKENS, KEY_VALUE_HEADS, HEAD_SIZE).astype(jnp.float32)
    live = jnp.arange(MOST_SEQ_PAGES * PAGE_TOKENS, dtype=jnp.int32)[None, :] < lengths[:, None]
    grouped_queries = queries.reshape(sequence_count, KEY_VALUE_HEADS, QUERY_HEADS // KEY_VALUE_HEADS, HEAD_SIZE).astype(jnp.float32)
    scale_factor = 1.0 / math.sqrt(HEAD_SIZE)
    scores = jnp.einsum('shgd,sthd->shgt', grouped_queries, every_key) * scale_factor
    scores = jnp.where(live[:, None, None, :], scores, -1e+30)
    self_score = jnp.einsum('fyvj,fyj->fyv', grouped_queries, fresh_token_keys.reshape(sequence_count, KEY_VALUE_HEADS, HEAD_SIZE).astype(jnp.float32)) * scale_factor
    highest = jnp.maximum(lax.optimization_barrier(jnp.max(scores, -1)), self_score)
    weights = jnp.exp(scores - highest[..., None])
    own_weight = jnp.exp(self_score - highest)
    total = lax.optimization_barrier(jnp.sum(weights, -1)) + own_weight
    probs = (weights / total[..., None]).astype(jnp.bfloat16)
    self_probability = (own_weight / total).astype(jnp.bfloat16)
    mixed_output = jnp.einsum('shgt,sthd->shgd', probs.astype(jnp.float32), every_value)
    mixed_output = mixed_output + self_probability.astype(jnp.float32)[..., None] * fresh_token_values.reshape(sequence_count, KEY_VALUE_HEADS, 1, HEAD_SIZE).astype(jnp.float32)
    return mixed_output.reshape(sequence_count, QUERY_HEADS * HEAD_SIZE).astype(jnp.bfloat16)

def reference(queries, fresh_token_keys, fresh_token_values, pooled_keys, pooled_values, lengths, page_order, hidden, out_weight, norm_gain, expert_ids, gate_weights, expert_gate_up, expert_down, mig_pages, mig_dest):
    row_width = KEY_VALUE_HEADS * HEAD_SIZE
    pool_k = pooled_keys.reshape(N_EP, DEVICE_POOL_PAGES, PAGE_TOKENS, row_width)
    pool_v = pooled_values.reshape(N_EP, DEVICE_POOL_PAGES, PAGE_TOKENS, row_width)
    inputs = (queries.reshape(N_EP, SEQ_DEV, QUERY_HEADS * HEAD_SIZE), fresh_token_keys.reshape(N_EP, SEQ_DEV, row_width), fresh_token_values.reshape(N_EP, SEQ_DEV, row_width), pool_k, pool_v, lengths, page_order)
    attn = lax.map(lambda items: attend_device(*items), inputs).reshape(INSTANCE_SEQS, QUERY_HEADS * HEAD_SIZE)
    proj = jnp.dot(attn, out_weight, preferred_element_type=jnp.float32)
    mid = (hidden.astype(jnp.float32) + proj).astype(jnp.bfloat16)
    mid_f = mid.astype(jnp.float32)
    normed = (mid_f * lax.rsqrt(lax.optimization_barrier(jnp.mean(mid_f * mid_f, -1, keepdims=True)) + 1e-06) * norm_gain).astype(jnp.bfloat16)
    flat_ids = expert_ids.reshape(-1)
    assign_all = INSTANCE_SEQS * TOPK
    owner_dev = jnp.arange(assign_all, dtype=jnp.int32) // (SEQ_DEV * TOPK)
    slots = N_EP * CAP
    gate_flat = gate_weights.reshape(-1)

    def one_expert(carry, items):
        expert, gate_up, down = items
        match = (flat_ids == expert).astype(jnp.int32)
        per_dev = match.reshape(N_EP, SEQ_DEV * TOPK)
        rank = (jnp.cumsum(per_dev, 1) - per_dev).astype(jnp.int32).reshape(-1)
        target = jnp.where(match > 0, owner_dev * CAP + rank, -1)
        select = (jnp.arange(slots, dtype=jnp.int32)[:, None] == target[None, :]).astype(jnp.float32)
        token_pick = select.reshape(slots, INSTANCE_SEQS, TOPK).sum(-1)
        rows = jnp.dot(token_pick.astype(jnp.bfloat16), normed, preferred_element_type=jnp.float32).astype(jnp.bfloat16)
        both = jnp.dot(rows, gate_up, preferred_element_type=jnp.float32)
        active = (jax.nn.silu(both[:, :FFW]) * both[:, FFW:]).astype(jnp.bfloat16)
        result = jnp.dot(active, down, preferred_element_type=jnp.float32).astype(jnp.bfloat16)
        mixing = (select * gate_flat[None, :]).reshape(slots, INSTANCE_SEQS, TOPK).sum(-1).T
        carry = carry + jnp.dot(mixing, result.astype(jnp.float32), precision=lax.Precision.HIGHEST)
        return (carry, None)
    start = jnp.zeros((INSTANCE_SEQS, D), jnp.float32)
    mixture, unused = lax.scan(one_expert, start, (jnp.arange(EXPERTS, dtype=jnp.int32), expert_gate_up, expert_down))
    layer_out = (mid.astype(jnp.float32) + mixture).astype(jnp.bfloat16)
    dest = mig_dest.reshape(N_EP, MIG_DEV)
    onehot = (dest[:, :, None] == jnp.arange(N_EP, dtype=jnp.int32)[None, None, :]).astype(jnp.float32)
    moved_k = jax.vmap(lambda pool, index: pool[index])(pool_k, mig_pages)
    moved_v = jax.vmap(lambda pool, index: pool[index])(pool_v, mig_pages)
    arrived_keys = jnp.einsum('smt,smpw->tspw', onehot, moved_k.astype(jnp.float32)).astype(jnp.bfloat16)
    arrived_values = jnp.einsum('smt,smpw->tspw', onehot, moved_v.astype(jnp.float32)).astype(jnp.bfloat16)
    arrived_keys = arrived_keys.reshape(N_EP * N_EP, PAGE_TOKENS, row_width)
    arrived_values = arrived_values.reshape(N_EP * N_EP, PAGE_TOKENS, row_width)
    return (layer_out, arrived_keys, arrived_values)
```

```python
import functools
import math

import jax
import jax.numpy as jnp
from jax import lax
from jax.experimental import pallas as pl
from jax.experimental.pallas import tpu as pltpu
from jax.sharding import PartitionSpec as P

QUERY_HEADS = 64
KEY_VALUE_HEADS = 4
HEAD_SIZE = 128
PAGE_TOKENS = 16
MOST_SEQ_PAGES = 16
SEQ_UNROLL = 4
PLANE = 4
MESH = pl.DeviceIdType.MESH


def attend_kernel(
    len_ref, order_ref, mig_page_ref, mig_dest_ref,
    q_ref, fk_ref, fv_ref, k_ref, v_ref,
    out_ref, mk_ref, mv_ref,
    ks, vs, fkf, fvf,
):
    pages = k_ref.shape[0]
    sequences = q_ref.shape[0]
    group = QUERY_HEADS // KEY_VALUE_HEADS
    width = KEY_VALUE_HEADS * HEAD_SIZE
    tokens = MOST_SEQ_PAGES * PAGE_TOKENS
    scale = 1.0 / math.sqrt(HEAD_SIZE)

    mk_ref[...] = jnp.zeros_like(mk_ref)
    mv_ref[...] = jnp.zeros_like(mv_ref)
    for i in range(mig_dest_ref.shape[0]):
        page, dest = mig_page_ref[0, i], mig_dest_ref[i, 0]
        mk_ref[dest] = k_ref[page]
        mv_ref[dest] = v_ref[page]

    fkf[...] = fk_ref[...].astype(jnp.float32)
    fvf[...] = fv_ref[...].astype(jnp.float32)
    row_head = lax.broadcasted_iota(jnp.int32, (QUERY_HEADS, width), 0) // group
    col_head = lax.broadcasted_iota(jnp.int32, (QUERY_HEADS, width), 1) // HEAD_SIZE
    diagonal = (row_head == col_head).astype(jnp.float32).astype(jnp.bfloat16)
    place = lax.broadcasted_iota(jnp.int32, (QUERY_HEADS, tokens), 1)

    def block(i, start):
        for u in range(SEQ_UNROLL):
            s = i * SEQ_UNROLL + u
            length = len_ref[0, s]
            for p in range(MOST_SEQ_PAGES):
                page = order_ref[0, jnp.minimum(start + p, pages - 1)]
                ks[u, p * PAGE_TOKENS:(p + 1) * PAGE_TOKENS, :] = k_ref[page]
                vs[u, p * PAGE_TOKENS:(p + 1) * PAGE_TOKENS, :] = v_ref[page]
            start = start + lax.div(length + (PAGE_TOKENS - 1), PAGE_TOKENS)
            q = q_ref[s]
            q_wide = jnp.concatenate([q] * KEY_VALUE_HEADS, axis=1) * diagonal
            scores = lax.dot_general(
                q_wide, ks[u], (((1,), (1,)), ((), ())), preferred_element_type=jnp.float32
            ) * scale
            scores = jnp.where(place < length, scores, -1e30)
            own = jnp.sum(
                q_wide.astype(jnp.float32) * fkf[pl.ds(s, 1), :], axis=1, keepdims=True
            ) * scale
            highest = jnp.maximum(jnp.max(scores, axis=1, keepdims=True), own)
            weights = jnp.exp(scores - highest)
            own_weight = jnp.exp(own - highest)
            total = jnp.sum(weights, axis=1, keepdims=True) + own_weight
            inverse = 1.0 / total
            probs = (weights * inverse).astype(jnp.bfloat16)
            own_prob = (own_weight * inverse).astype(jnp.bfloat16).astype(jnp.float32)
            mixed = jnp.dot(probs, vs[u], preferred_element_type=jnp.float32)
            mixed = mixed + own_prob * fvf[pl.ds(s, 1), :]
            out_ref[s] = jnp.concatenate(
                [
                    mixed[h * group:(h + 1) * group, h * HEAD_SIZE:(h + 1) * HEAD_SIZE]
                    for h in range(KEY_VALUE_HEADS)
                ],
                axis=0,
            ).astype(jnp.bfloat16)
        return start

    lax.fori_loop(0, sequences // SEQ_UNROLL, block, jnp.int32(0))


def attend(queries, fresh_keys, fresh_values, pooled_keys, pooled_values, lengths, page_order,
           mig_pages, mig_dest, n):
    sequences = queries.shape[0]
    width = KEY_VALUE_HEADS * HEAD_SIZE
    tokens = MOST_SEQ_PAGES * PAGE_TOKENS
    smem = pl.BlockSpec(memory_space=pltpu.SMEM)
    vmem = pl.BlockSpec(memory_space=pltpu.VMEM)
    page = (PAGE_TOKENS, width)
    return pl.pallas_call(
        attend_kernel,
        out_shape=(
            jax.ShapeDtypeStruct((sequences, QUERY_HEADS, HEAD_SIZE), jnp.bfloat16),
            jax.ShapeDtypeStruct((n,) + page, jnp.bfloat16),
            jax.ShapeDtypeStruct((n,) + page, jnp.bfloat16),
        ),
        in_specs=[smem] * 4 + [vmem] * 5,
        out_specs=(vmem,) * 3,
        scratch_shapes=[
            pltpu.VMEM((SEQ_UNROLL, tokens, width), jnp.bfloat16),
            pltpu.VMEM((SEQ_UNROLL, tokens, width), jnp.bfloat16),
            pltpu.VMEM((sequences, width), jnp.float32),
            pltpu.VMEM((sequences, width), jnp.float32),
        ],
        compiler_params=pltpu.CompilerParams(vmem_limit_bytes=40 * 1024 * 1024),
    )(lengths, page_order, mig_pages, mig_dest,
      queries.reshape(sequences, QUERY_HEADS, HEAD_SIZE), fresh_keys, fresh_values,
      pooled_keys, pooled_values)


def layer_kernel(
    n, attn_ref, gate_ref, hidden_ref, gain_ref, mk_ref, mv_ref, wo_hbm, wgu_hbm, wd_hbm,
    out_ref, ak_ref, av_ref,
    wo, wgu, wd, heads, gates, part, crecv, yrecv, zrecv, rows, act, mid, acc,
    wsem, asend, arecv, gsend, grecv, ksend, krecv, vsend, vrecv, rs, nsz, nsy, nsc, nrecv,
):
    G = n // PLANE
    me = lax.axis_index("ep")
    g = lax.div(me, PLANE)
    lane = lax.rem(me, PLANE)
    b = lax.div(lane, 2)
    c = lax.rem(lane, 2)
    S = hidden_ref.shape[0]
    D = hidden_ref.shape[1]
    FFW = wd_hbm.shape[0]
    block_rows = PLANE * S

    def dev(gg, bb, cc):
        return {"ep": gg * PLANE + bb * 2 + cc}

    def remote(src, dst, send, recv, to):
        return pltpu.make_async_remote_copy(
            src_ref=src, dst_ref=dst, send_sem=send, recv_sem=recv, device_id=to,
            device_id_type=MESH,
        )

    load_wo = pltpu.make_async_copy(wo_hbm, wo, wsem.at[0])
    load_wgu = pltpu.make_async_copy(wgu_hbm, wgu, wsem.at[1])
    load_wd = pltpu.make_async_copy(wd_hbm, wd, wsem.at[2])
    load_wo.start()
    load_wgu.start()
    load_wd.start()
    own_k = pltpu.make_async_copy(mk_ref.at[me], ak_ref.at[me], wsem.at[3])
    own_v = pltpu.make_async_copy(mv_ref.at[me], av_ref.at[me], wsem.at[4])
    own_k.start()
    own_v.start()
    heads[me] = attn_ref[me]
    gates[me] = gate_ref[...]

    barrier = pltpu.get_barrier_semaphore()

    @pl.loop(1, n)
    def _(i):
        pl.semaphore_signal(
            barrier, inc=1, device_id={"ep": lax.rem(me + i, n)}, device_id_type=MESH
        )

    pl.semaphore_wait(barrier, n - 1)

    def peer_of(k):
        i = lax.div(k, PLANE) + 1
        return lax.rem(g + (G - i), G) * PLANE + lax.rem(lane + 1 + lax.rem(k, PLANE), PLANE)

    def attn_copy(slot, peer):
        return remote(attn_ref.at[peer], heads.at[slot], asend.at[peer], arecv.at[slot],
                      {"ep": peer})

    def gate_copy(slot, peer):
        return remote(gate_ref, gates.at[slot], gsend.at[peer], grecv.at[slot], {"ep": peer})

    def key_copy(slot, peer):
        return remote(mk_ref.at[peer], ak_ref.at[slot], ksend.at[peer], krecv.at[slot],
                      {"ep": peer})

    def value_copy(slot, peer):
        return remote(mv_ref.at[peer], av_ref.at[slot], vsend.at[peer], vrecv.at[slot],
                      {"ep": peer})

    @pl.loop(0, n - 1)
    def _(k):
        attn_copy(me, peer_of(k)).start()

    @pl.loop(0, n - 1)
    def _(k):
        gate_copy(me, peer_of(k)).start()
        key_copy(me, peer_of(k)).start()
        value_copy(me, peer_of(k)).start()

    def c_copy(r, gi):
        return remote(part.at[gi, :, 1 - c], crecv.at[r, gi], rs.at[r, 0, gi], rs.at[r, 1, gi],
                      dev(g, b, 1 - c))

    def y_copy(r, gi):
        return remote(crecv.at[r, gi, 1 - b], yrecv.at[r, gi], rs.at[r, 2, gi], rs.at[r, 3, gi],
                      dev(g, 1 - b, c))

    def z_copy(r, gi, slot):
        return remote(yrecv.at[r, gi], zrecv.at[r, slot], rs.at[r, 4, gi], rs.at[r, 5, slot],
                      dev(gi, b, c))

    def core_stage(r, gi):
        c_copy(r, gi).wait_recv()
        for bb in range(2):
            crecv[r, gi, bb] = (
                part[gi, bb, c].astype(jnp.float32) + crecv[r, gi, bb].astype(jnp.float32)
            ).astype(jnp.bfloat16)
        y_copy(r, gi).start()

    def y_stage(r, gi):
        y_copy(r, gi).wait_recv()
        yrecv[r, gi] = (
            crecv[r, gi, b].astype(jnp.float32) + yrecv[r, gi].astype(jnp.float32)
        ).astype(jnp.bfloat16)

    def collect(r):
        acc[...] = yrecv[r, g].astype(jnp.float32)

        @pl.loop(1, G)
        def _(i):
            src = lax.rem(g + i, G)
            z_copy(r, g, src).wait_recv()
            acc[...] += zrecv[r, src].astype(jnp.float32)

    load_wo.wait()
    tile = 1024

    @pl.loop(0, G + 2)
    def _(t):
        @pl.when(t < G)
        def _():
            gi = lax.rem(g + 1 + t, G)
            for j in range(PLANE):
                src = gi * PLANE + j

                @pl.when(src != me)
                def _():
                    attn_copy(src, src).wait_recv()

            left = heads[pl.ds(gi * PLANE, PLANE)].reshape(block_rows, heads.shape[2])
            for j in range(D // tile):
                part[gi, :, :, :, j * tile:(j + 1) * tile] = jnp.dot(
                    left, wo[:, j * tile:(j + 1) * tile], preferred_element_type=jnp.float32
                ).astype(jnp.bfloat16).reshape(2, 2, S, tile)
            c_copy(0, gi).start()

        @pl.when((t >= 1) & (t <= G))
        def _():
            core_stage(0, lax.rem(g + t, G))

        @pl.when(t >= 2)
        def _():
            gi = lax.rem(g + t - 1, G)
            y_stage(0, gi)

            @pl.when(t <= G)
            def _():
                z_copy(0, gi, g).start()

    collect(0)
    middle = (hidden_ref[...].astype(jnp.float32) + acc[...]).astype(jnp.bfloat16)
    mid[...] = middle
    middle = middle.astype(jnp.float32)
    scale = lax.rsqrt(jnp.mean(middle * middle, axis=1, keepdims=True) + 1e-06)
    rows[g, b, c] = (middle * scale * gain_ref[...]).astype(jnp.bfloat16)

    def row_copy(gg, bb, cc, send, to):
        slot = rows.at[gg, bb, cc]
        return remote(slot, slot, send, nrecv.at[gg, bb, cc], to)

    def rows_to_z(target):
        return row_copy(g, b, c, nsz.at[target], dev(target, b, c))

    def rows_to_y(gg):
        return row_copy(gg, b, c, nsy.at[gg], dev(g, 1 - b, c))

    def rows_to_core(gg, bb):
        return row_copy(gg, bb, c, nsc.at[gg, bb], dev(g, b, 1 - c))

    def arrival(gg, bb, cc):
        return row_copy(gg, bb, cc, nsy.at[gg], dev(g, b, 1 - c))

    rows_to_core(g, b).start()
    rows_to_y(g).start()

    @pl.loop(1, G)
    def _(i):
        rows_to_z(lax.rem(g + (G - i), G)).start()

    @pl.loop(0, n - 1)
    def _(k):
        peer = peer_of(k)
        gate_copy(peer, peer).wait_recv()

    @pl.loop(0, G)
    def _(gi):
        c_copy(0, gi).wait_send()

    load_wgu.wait()
    load_wd.wait()
    half = 256

    @pl.loop(0, G + 2)
    def _(t):
        @pl.when(t + 1 < G)
        def _():
            gi = lax.rem(g + t + 1, G)
            arrival(gi, b, c).wait_recv()
            rows_to_y(gi).start()
            rows_to_core(gi, b).start()

        @pl.when(t < G)
        def _():
            gi = lax.rem(g + t, G)
            arrival(gi, 1 - b, c).wait_recv()
            rows_to_core(gi, 1 - b).start()
            arrival(gi, b, 1 - c).wait_recv()
            arrival(gi, 1 - b, 1 - c).wait_recv()

            @pl.loop(0, FFW // half)
            def _(j):
                left = rows[gi].reshape(block_rows, D)
                at = pl.multiple_of(j * half, half)
                gate = jnp.dot(left, wgu[:, pl.ds(at, half)], preferred_element_type=jnp.float32)
                up = jnp.dot(left, wgu[:, pl.ds(FFW + at, half)],
                             preferred_element_type=jnp.float32)
                act[:, pl.ds(at, half)] = (gate * jax.nn.sigmoid(gate) * up).astype(jnp.bfloat16)

            table = gates[pl.ds(gi * PLANE, PLANE)].reshape(block_rows, gates.shape[2])
            column = lax.broadcasted_iota(jnp.int32, table.shape, 1)
            chosen = jnp.sum(jnp.where(column == me, table, 0.0), axis=1, keepdims=True)
            for j in range(D // tile):
                y = jnp.dot(act[...], wd[:, j * tile:(j + 1) * tile],
                            preferred_element_type=jnp.float32)
                y = y.astype(jnp.bfloat16).astype(jnp.float32) * chosen
                part[gi, :, :, :, j * tile:(j + 1) * tile] = y.astype(jnp.bfloat16).reshape(
                    2, 2, S, tile
                )
            c_copy(1, gi).start()

        @pl.when((t >= 1) & (t <= G))
        def _():
            core_stage(1, lax.rem(g + t - 1, G))

        @pl.when(t >= 2)
        def _():
            gi = lax.rem(g + t - 2, G)
            y_stage(1, gi)

            @pl.when(t >= 3)
            def _():
                z_copy(1, gi, g).start()

    collect(1)
    out_ref[...] = (mid[...].astype(jnp.float32) + acc[...]).astype(jnp.bfloat16)

    own_k.wait()
    own_v.wait()

    @pl.loop(0, n - 1)
    def _(k):
        peer = peer_of(k)
        attn_copy(me, peer).wait_send()
        gate_copy(me, peer).wait_send()
        key_copy(me, peer).wait_send()
        value_copy(me, peer).wait_send()
        key_copy(peer, peer).wait_recv()
        value_copy(peer, peer).wait_recv()

    @pl.loop(0, G)
    def _(gi):
        c_copy(1, gi).wait_send()
        rows_to_y(gi).wait_send()
        rows_to_core(gi, 0).wait_send()
        rows_to_core(gi, 1).wait_send()
        for r in range(2):
            y_copy(r, gi).wait_send()

    @pl.loop(1, G)
    def _(i):
        gi = lax.rem(g + i, G)
        rows_to_z(gi).wait_send()
        for r in range(2):
            z_copy(r, gi, g).wait_send()


def layer(n, attn, gate, hidden, gain, mk, mv, wo, wgu, wd):
    G = n // PLANE
    S, D = hidden.shape
    FFW = wd.shape[0]
    vmem = pl.BlockSpec(memory_space=pltpu.VMEM)
    anywhere = pl.BlockSpec(memory_space=pl.ANY)
    bf16 = jnp.bfloat16
    dma = pltpu.SemaphoreType.DMA
    return pl.pallas_call(
        functools.partial(layer_kernel, n),
        out_shape=(
            jax.ShapeDtypeStruct(hidden.shape, bf16),
            jax.ShapeDtypeStruct(mk.shape, bf16),
            jax.ShapeDtypeStruct(mv.shape, bf16),
        ),
        in_specs=[vmem] * 4 + [anywhere] * 5,
        out_specs=(vmem, anywhere, anywhere),
        scratch_shapes=[
            pltpu.VMEM(wo.shape, bf16),
            pltpu.VMEM(wgu.shape, bf16),
            pltpu.VMEM(wd.shape, bf16),
            pltpu.VMEM(attn.shape, bf16),
            pltpu.VMEM((n,) + gate.shape, jnp.float32),
            pltpu.VMEM((G, 2, 2, S, D), bf16),
            pltpu.VMEM((2, G, 2, S, D), bf16),
            pltpu.VMEM((2, G, S, D), bf16),
            pltpu.VMEM((2, G, S, D), bf16),
            pltpu.VMEM((G, 2, 2, S, D), bf16),
            pltpu.VMEM((PLANE * S, FFW), bf16),
            pltpu.VMEM((S, D), bf16),
            pltpu.VMEM((S, D), jnp.float32),
            dma((5,)),
            dma((n,)), dma((n,)), dma((n,)), dma((n,)),
            dma((n,)), dma((n,)), dma((n,)), dma((n,)),
            dma((2, 6, G)),
            dma((G,)), dma((G,)), dma((G, 2)), dma((G, 2, 2)),
        ],
        compiler_params=pltpu.CompilerParams(
            collective_id=0, has_side_effects=True, vmem_limit_bytes=63 * 1024 * 1024
        ),
    )(attn, gate, hidden, gain, mk, mv, wo, wgu, wd)


def on_device(
    queries, fresh_token_keys, fresh_token_values, pooled_keys, pooled_values, lengths, page_order,
    hidden, out_weight, norm_gain, expert_ids, gate_weights, expert_gate_up, expert_down,
    mig_pages, mig_dest,
):
    n = lax.axis_size("ep")
    sequences = queries.shape[0]
    attended, mk, mv = attend(
        queries, fresh_token_keys, fresh_token_values, pooled_keys, pooled_values, lengths,
        page_order, mig_pages, mig_dest, n,
    )
    attended = attended.reshape(sequences, n, out_weight.shape[0]).transpose(1, 0, 2)
    lanes = jnp.arange(128, dtype=jnp.int32)
    gate = jnp.sum(
        jnp.where(expert_ids[:, :, None] == lanes, gate_weights[:, :, None], 0.0), axis=1
    )
    return layer(
        n, attended, gate, hidden, norm_gain[None, :], mk, mv, out_weight, expert_gate_up[0],
        expert_down[0],
    )


def solution(mesh):
    return jax.shard_map(
        on_device,
        mesh=mesh,
        in_specs=(
            P(("parts", "ep"), None),
            P(("parts", "ep"), None),
            P(("parts", "ep"), None),
            P(("parts", "ep"), None, None),
            P(("parts", "ep"), None, None),
            P(("parts", "ep"), None),
            P(("parts", "ep"), None),
            P(("parts", "ep"), None),
            P("ep", None),
            P(),
            P(("parts", "ep"), None),
            P(("parts", "ep"), None),
            P("ep", None, None),
            P("ep", None, None),
            P(("parts", "ep"), None),
            P(("parts", "ep"), None),
        ),
        out_specs=(
            P(("parts", "ep"), None),
            P(("parts", "ep"), None, None),
            P(("parts", "ep"), None, None),
        ),
        check_vma=False,
    )
```

```python
import functools
import math

import jax
import jax.numpy as jnp
from jax import lax
from jax.experimental import pallas as pl
from jax.experimental.pallas import tpu as pltpu
from jax.sharding import PartitionSpec as P

QUERY_HEADS = 64
KEY_VALUE_HEADS = 4
HEAD_SIZE = 128
PAGE_TOKENS = 16
MOST_SEQ_PAGES = 16
SEQ_UNROLL = 4
PLANE = 4
MESH = pl.DeviceIdType.MESH


def layer_kernel(
    n, len_ref, order_ref, mig_page_ref, mig_dest_ref, ids_ref, weights_ref,
    q_hbm, fk_hbm, fv_hbm, k_hbm, v_hbm, hidden_hbm, gain_hbm, wo_hbm, wgu_hbm, wd_hbm,
    out_ref, ak_ref, av_ref,
    wo, wgu, wd, heads, gates, part, crecv, yrecv, zrecv, rows, act, mid, acc,
    q_in, qs, attn_ref, ks, vs, fresh, fkf, fvf, mk_ref, mv_ref, gate_ref, hidden_ref, gain_ref,
    wsem, asend, arecv, gsend, grecv, ksend, krecv, vsend, vrecv, rs, nsz, nsy, nsc, nrecv,
):
    G = n // PLANE
    me = lax.axis_index("ep")
    g = lax.div(me, PLANE)
    lane = lax.rem(me, PLANE)
    b = lax.div(lane, 2)
    c = lax.rem(lane, 2)
    S = hidden_ref.shape[0]
    D = hidden_ref.shape[1]
    FFW = wd_hbm.shape[0]
    block_rows = PLANE * S

    def dev(gg, bb, cc):
        return {"ep": gg * PLANE + bb * 2 + cc}

    def remote(src, dst, send, recv, to):
        return pltpu.make_async_remote_copy(
            src_ref=src, dst_ref=dst, send_sem=send, recv_sem=recv, device_id=to,
            device_id_type=MESH,
        )

    pages = k_hbm.shape[0]
    width = KEY_VALUE_HEADS * HEAD_SIZE
    kpool = wgu.at[0:pages, :, 0:width]
    vpool = wgu.at[0:pages, :, width:2 * width]
    load_k = pltpu.make_async_copy(k_hbm, kpool, wsem.at[0])
    load_v = pltpu.make_async_copy(v_hbm, vpool, wsem.at[1])
    load_q = pltpu.make_async_copy(q_hbm, q_in, wsem.at[2])
    load_fk = pltpu.make_async_copy(fk_hbm, fresh.at[0], wsem.at[3])
    load_fv = pltpu.make_async_copy(fv_hbm, fresh.at[1], wsem.at[4])
    load_wo = pltpu.make_async_copy(wo_hbm, wo, wsem.at[5])
    load_wd = pltpu.make_async_copy(wd_hbm, wd, wsem.at[6])
    load_hidden = pltpu.make_async_copy(hidden_hbm, hidden_ref, wsem.at[7])
    load_gain = pltpu.make_async_copy(gain_hbm, gain_ref, wsem.at[8])
    load_wgu = pltpu.make_async_copy(wgu_hbm, wgu, wsem.at[9])
    own_k = pltpu.make_async_copy(mk_ref.at[me], ak_ref.at[me], wsem.at[10])
    own_v = pltpu.make_async_copy(mv_ref.at[me], av_ref.at[me], wsem.at[11])
    for load in (load_k, load_v, load_q, load_fk, load_fv, load_wo, load_wd, load_hidden,
                 load_gain):
        load.start()

    barrier = pltpu.get_barrier_semaphore()

    @pl.loop(1, n)
    def _(i):
        pl.semaphore_signal(
            barrier, inc=1, device_id={"ep": lax.rem(me + i, n)}, device_id_type=MESH
        )

    experts = lax.broadcasted_iota(jnp.int32, (128, S), 0)
    table = jnp.zeros((128, S), jnp.float32)
    for k in range(ids_ref.shape[0]):
        table = table + jnp.where(experts == ids_ref[k:k + 1, :], weights_ref[k:k + 1, :], 0.0)
    table = jnp.concatenate([table, jnp.zeros((128, 128 - S), jnp.float32)], axis=1)
    gate_ref[...] = table.T[0:S, :]
    gates[me] = gate_ref[...]

    def near(t):
        closest = jnp.minimum(g, G - 1 - g)
        away = lax.div(t + 1, 2)
        side = jnp.where(lax.rem(t, 2) == 1, g - away, g + away)
        rest = jnp.where(g + g <= G - 1, t, G - 1 - t)
        return jnp.where(t <= closest + closest, side, rest)

    def peer_of(k):
        plane = near(G - 1 - lax.div(k, PLANE))
        return plane * PLANE + lax.rem(lane + 1 + lax.rem(k, PLANE), PLANE)

    half_rows = S // 2

    def attn_copy(slot, peer, part_no):
        at = pl.ds(pl.multiple_of(part_no * half_rows, half_rows), half_rows)
        return remote(attn_ref.at[peer, at], heads.at[slot, at], asend.at[part_no, peer],
                      arecv.at[part_no, slot], {"ep": peer})

    def gate_copy(slot, peer):
        return remote(gate_ref, gates.at[slot], gsend.at[peer], grecv.at[slot], {"ep": peer})

    def key_copy(slot, peer):
        return remote(mk_ref.at[peer], ak_ref.at[slot], ksend.at[peer], krecv.at[slot],
                      {"ep": peer})

    def value_copy(slot, peer):
        return remote(mv_ref.at[peer], av_ref.at[slot], vsend.at[peer], vrecv.at[slot],
                      {"ep": peer})

    def stage_pages(dest):
        page, found = jnp.int32(0), jnp.int32(0)
        for i in range(mig_page_ref.shape[1]):
            same = mig_dest_ref[0, i] == dest
            page = jnp.where(same, mig_page_ref[0, i], page)
            found = jnp.where(same, 1, found)
        keep = jnp.full((PAGE_TOKENS, width), found, jnp.int32) == 1
        zero = jnp.zeros((PAGE_TOKENS, width), jnp.float32)
        for pool, staged in ((0, mk_ref), (width, mv_ref)):
            rows_of = wgu[page, :, pool:pool + width].astype(jnp.float32)
            staged[dest] = jnp.where(keep, rows_of, zero).astype(jnp.bfloat16)

    load_k.wait()
    load_v.wait()
    stage_pages(me)
    own_k.start()
    own_v.start()
    pl.semaphore_wait(barrier, n - 1)

    @pl.loop(0, n - 1)
    def _(k):
        peer = peer_of(k)
        stage_pages(peer)
        key_copy(me, peer).start()
        value_copy(me, peer).start()
        gate_copy(me, peer).start()

    load_q.wait()
    load_fk.wait()
    load_fv.wait()
    for h in range(QUERY_HEADS):
        qs[pl.ds(h, S, stride=QUERY_HEADS), :] = q_in[
            :, h * HEAD_SIZE:(h + 1) * HEAD_SIZE
        ].astype(jnp.float32)
    fkf[...] = fresh[0].astype(jnp.float32)
    fvf[...] = fresh[1].astype(jnp.float32)

    group = QUERY_HEADS // KEY_VALUE_HEADS
    tokens = MOST_SEQ_PAGES * PAGE_TOKENS
    score_scale = 1.0 / math.sqrt(HEAD_SIZE)
    row_head = lax.broadcasted_iota(jnp.int32, (QUERY_HEADS, width), 0) // group
    col_head = lax.broadcasted_iota(jnp.int32, (QUERY_HEADS, width), 1) // HEAD_SIZE
    diagonal = (row_head == col_head).astype(jnp.float32).astype(jnp.bfloat16)
    place = lax.broadcasted_iota(jnp.int32, (QUERY_HEADS, tokens), 1)

    def attend_some(part_no, i, start):
        for u in range(SEQ_UNROLL):
            s = part_no * half_rows + i * SEQ_UNROLL + u
            length = len_ref[0, s]
            for p in range(MOST_SEQ_PAGES):
                page = order_ref[0, jnp.minimum(start + p, pages - 1)]
                ks[u, p * PAGE_TOKENS:(p + 1) * PAGE_TOKENS, :] = wgu[page, :, 0:width]
                vs[u, p * PAGE_TOKENS:(p + 1) * PAGE_TOKENS, :] = wgu[page, :, width:2 * width]
            start = start + lax.div(length + (PAGE_TOKENS - 1), PAGE_TOKENS)
            s_rows = pl.ds(pl.multiple_of(s * QUERY_HEADS, QUERY_HEADS), QUERY_HEADS)
            q = qs[s_rows, :].astype(jnp.bfloat16)
            q_wide = jnp.concatenate([q] * KEY_VALUE_HEADS, axis=1) * diagonal
            scores = lax.dot_general(
                q_wide, ks[u], (((1,), (1,)), ((), ())), preferred_element_type=jnp.float32
            ) * score_scale
            scores = jnp.where(place < length, scores, -1e30)
            own = jnp.sum(
                q_wide.astype(jnp.float32) * fkf[pl.ds(s, 1), :], axis=1, keepdims=True
            ) * score_scale
            highest = jnp.maximum(jnp.max(scores, axis=1, keepdims=True), own)
            weights = jnp.exp(scores - highest)
            own_weight = jnp.exp(own - highest)
            total = jnp.sum(weights, axis=1, keepdims=True) + own_weight
            inverse = 1.0 / total
            probs = (weights * inverse).astype(jnp.bfloat16)
            own_prob = (own_weight * inverse).astype(jnp.bfloat16).astype(jnp.float32)
            mixed = jnp.dot(probs, vs[u], preferred_element_type=jnp.float32)
            mixed = mixed + own_prob * fvf[pl.ds(s, 1), :]
            qs[s_rows, :] = jnp.concatenate(
                [
                    mixed[h * group:(h + 1) * group, h * HEAD_SIZE:(h + 1) * HEAD_SIZE]
                    for h in range(KEY_VALUE_HEADS)
                ],
                axis=0,
            )
        return start

    some = half_rows // SEQ_UNROLL
    head_share = QUERY_HEADS // n

    def attend_half(part_no, start):
        start = lax.fori_loop(0, some, functools.partial(attend_some, part_no), start)
        at = pl.ds(pl.multiple_of(part_no * half_rows, half_rows), half_rows)
        first = part_no * (half_rows * QUERY_HEADS)
        for h in range(QUERY_HEADS):
            d, j = h // head_share, h % head_share
            attn_ref[d, at, j * HEAD_SIZE:(j + 1) * HEAD_SIZE] = qs[
                pl.ds(first + h, half_rows, stride=QUERY_HEADS), :
            ].astype(jnp.bfloat16)

        @pl.loop(0, n - 1)
        def _(k):
            attn_copy(me, peer_of(k), part_no).start()

        return start

    lax.fori_loop(0, 2, attend_half, jnp.int32(0))
    heads[me] = attn_ref[me]
    load_wgu.start()

    def c_copy(r, gi):
        return remote(part.at[gi, :, 1 - c], crecv.at[r, gi], rs.at[r, 0, gi], rs.at[r, 1, gi],
                      dev(g, b, 1 - c))

    def y_copy(r, gi):
        return remote(crecv.at[r, gi, 1 - b], yrecv.at[r, gi], rs.at[r, 2, gi], rs.at[r, 3, gi],
                      dev(g, 1 - b, c))

    def z_copy(r, gi, slot):
        return remote(yrecv.at[r, gi], zrecv.at[r, slot], rs.at[r, 4, gi], rs.at[r, 5, slot],
                      dev(gi, b, c))

    def core_stage(r, gi):
        c_copy(r, gi).wait_recv()
        for bb in range(2):
            crecv[r, gi, bb] = (
                part[gi, bb, c].astype(jnp.float32) + crecv[r, gi, bb].astype(jnp.float32)
            ).astype(jnp.bfloat16)
        y_copy(r, gi).start()

    def y_stage(r, gi):
        y_copy(r, gi).wait_recv()
        yrecv[r, gi] = (
            crecv[r, gi, b].astype(jnp.float32) + yrecv[r, gi].astype(jnp.float32)
        ).astype(jnp.bfloat16)

    def collect(r):
        acc[...] = yrecv[r, g].astype(jnp.float32)

        @pl.loop(1, G)
        def _(i):
            src = lax.rem(g + i, G)
            z_copy(r, g, src).wait_recv()
            acc[...] += zrecv[r, src].astype(jnp.float32)

    load_wo.wait()
    tile = 1024

    @pl.loop(0, G + 2)
    def _(t):
        @pl.when(t < G)
        def _():
            gi = near(G - 1 - t)
            for j in range(PLANE):
                src = gi * PLANE + j

                @pl.when(src != me)
                def _():
                    attn_copy(src, src, 0).wait_recv()
                    attn_copy(src, src, 1).wait_recv()

            left = heads[pl.ds(gi * PLANE, PLANE)].reshape(block_rows, heads.shape[2])
            for j in range(D // tile):
                part[gi, :, :, :, j * tile:(j + 1) * tile] = jnp.dot(
                    left, wo[:, j * tile:(j + 1) * tile], preferred_element_type=jnp.float32
                ).astype(jnp.bfloat16).reshape(2, 2, S, tile)
            c_copy(0, gi).start()

        @pl.when((t >= 1) & (t <= G))
        def _():
            core_stage(0, near(G - t))

        @pl.when(t >= 2)
        def _():
            gi = near(G + 1 - t)
            y_stage(0, gi)

            @pl.when(t <= G)
            def _():
                z_copy(0, gi, g).start()

    collect(0)
    load_hidden.wait()
    load_gain.wait()
    middle = (hidden_ref[...].astype(jnp.float32) + acc[...]).astype(jnp.bfloat16)
    mid[...] = middle
    middle = middle.astype(jnp.float32)
    scale = lax.rsqrt(jnp.mean(middle * middle, axis=1, keepdims=True) + 1e-06)
    rows[g, b, c] = (middle * scale * gain_ref[...]).astype(jnp.bfloat16)

    def row_copy(gg, bb, cc, send, to):
        slot = rows.at[gg, bb, cc]
        return remote(slot, slot, send, nrecv.at[gg, bb, cc], to)

    def rows_to_z(gg, step):
        return row_copy(gg, b, c, nsz.at[gg, (step + 1) // 2], dev(g + step, b, c))

    def pass_on(gg, act_on):
        @pl.when((gg <= g) & (g + 1 < G))
        def _():
            act_on(rows_to_z(gg, 1))

        @pl.when((gg >= g) & (g >= 1))
        def _():
            act_on(rows_to_z(gg, -1))

    def rows_to_y(gg):
        return row_copy(gg, b, c, nsy.at[gg], dev(g, 1 - b, c))

    def rows_to_core(gg, bb):
        return row_copy(gg, bb, c, nsc.at[gg, bb], dev(g, b, 1 - c))

    def arrival(gg, bb, cc):
        return row_copy(gg, bb, cc, nsy.at[gg], dev(g, b, 1 - c))

    rows_to_core(g, b).start()
    rows_to_y(g).start()

    pass_on(g, lambda copy: copy.start())

    @pl.loop(0, n - 1)
    def _(k):
        peer = peer_of(k)
        gate_copy(peer, peer).wait_recv()

    @pl.loop(0, G)
    def _(gi):
        c_copy(0, gi).wait_send()

    load_wgu.wait()
    load_wd.wait()
    half = 256

    @pl.loop(0, G + 2)
    def _(t):
        @pl.when(t + 1 < G)
        def _():
            gi = near(t + 1)
            arrival(gi, b, c).wait_recv()
            pass_on(gi, lambda copy: copy.start())
            rows_to_y(gi).start()
            rows_to_core(gi, b).start()

        @pl.when(t < G)
        def _():
            gi = near(t)
            arrival(gi, 1 - b, c).wait_recv()
            rows_to_core(gi, 1 - b).start()
            arrival(gi, b, 1 - c).wait_recv()
            arrival(gi, 1 - b, 1 - c).wait_recv()

            @pl.loop(0, FFW // half)
            def _(j):
                left = rows[gi].reshape(block_rows, D)
                at = pl.multiple_of(j * half, half)
                gate = jnp.dot(left, wgu[:, :, pl.ds(at, half)].reshape(D, half),
                               preferred_element_type=jnp.float32)
                up = jnp.dot(left, wgu[:, :, pl.ds(FFW + at, half)].reshape(D, half),
                             preferred_element_type=jnp.float32)
                act[:, pl.ds(at, half)] = (gate * jax.nn.sigmoid(gate) * up).astype(jnp.bfloat16)

            table = gates[pl.ds(gi * PLANE, PLANE)].reshape(block_rows, gates.shape[2])
            column = lax.broadcasted_iota(jnp.int32, table.shape, 1)
            chosen = jnp.sum(jnp.where(column == me, table, 0.0), axis=1, keepdims=True)
            for j in range(D // tile):
                y = jnp.dot(act[...], wd[:, j * tile:(j + 1) * tile],
                            preferred_element_type=jnp.float32)
                y = y.astype(jnp.bfloat16).astype(jnp.float32) * chosen
                part[gi, :, :, :, j * tile:(j + 1) * tile] = y.astype(jnp.bfloat16).reshape(
                    2, 2, S, tile
                )
            c_copy(1, gi).start()

        @pl.when((t >= 1) & (t <= G))
        def _():
            core_stage(1, near(t - 1))

        @pl.when(t >= 2)
        def _():
            gi = near(t - 2)
            y_stage(1, gi)

            @pl.when(t >= 3)
            def _():
                z_copy(1, gi, g).start()

    collect(1)
    out_ref[...] = (mid[...].astype(jnp.float32) + acc[...]).astype(jnp.bfloat16)

    own_k.wait()
    own_v.wait()

    @pl.loop(0, n - 1)
    def _(k):
        peer = peer_of(k)
        attn_copy(me, peer, 0).wait_send()
        attn_copy(me, peer, 1).wait_send()
        gate_copy(me, peer).wait_send()
        key_copy(me, peer).wait_send()
        value_copy(me, peer).wait_send()
        key_copy(peer, peer).wait_recv()
        value_copy(peer, peer).wait_recv()

    @pl.loop(0, G)
    def _(gi):
        c_copy(1, gi).wait_send()
        rows_to_y(gi).wait_send()
        rows_to_core(gi, 0).wait_send()
        rows_to_core(gi, 1).wait_send()
        pass_on(gi, lambda copy: copy.wait_send())
        for r in range(2):
            y_copy(r, gi).wait_send()

    @pl.loop(1, G)
    def _(i):
        gi = lax.rem(g + i, G)
        for r in range(2):
            z_copy(r, gi, g).wait_send()


def layer(n, lengths, page_order, mig_pages, mig_dest, ids, weights, queries, fresh_keys,
          fresh_values, keys, values, hidden, gain, wo, wgu, wd):
    G = n // PLANE
    S, D = hidden.shape
    FFW = wd.shape[0]
    width = KEY_VALUE_HEADS * HEAD_SIZE
    tokens = MOST_SEQ_PAGES * PAGE_TOKENS
    pages = (n, PAGE_TOKENS, width)
    smem = pl.BlockSpec(memory_space=pltpu.SMEM)
    vmem = pl.BlockSpec(memory_space=pltpu.VMEM)
    anywhere = pl.BlockSpec(memory_space=pl.ANY)
    bf16 = jnp.bfloat16
    dma = pltpu.SemaphoreType.DMA
    return pl.pallas_call(
        functools.partial(layer_kernel, n),
        out_shape=(
            jax.ShapeDtypeStruct(hidden.shape, bf16),
            jax.ShapeDtypeStruct(pages, bf16),
            jax.ShapeDtypeStruct(pages, bf16),
        ),
        in_specs=[smem] * 4 + [vmem] * 2 + [anywhere] * 10,
        out_specs=(vmem, anywhere, anywhere),
        scratch_shapes=[
            pltpu.VMEM(wo.shape, bf16),
            pltpu.VMEM(wgu.shape, bf16),
            pltpu.VMEM(wd.shape, bf16),
            pltpu.VMEM((n, S, wo.shape[0]), bf16),
            pltpu.VMEM((n, S, 128), jnp.float32),
            pltpu.VMEM((G, 2, 2, S, D), bf16),
            pltpu.VMEM((2, G, 2, S, D), bf16),
            pltpu.VMEM((2, G, S, D), bf16),
            pltpu.VMEM((2, G, S, D), bf16),
            pltpu.VMEM((G, 2, 2, S, D), bf16),
            pltpu.VMEM((PLANE * S, FFW), bf16),
            pltpu.VMEM((S, D), bf16),
            pltpu.VMEM((S, D), jnp.float32),
            pltpu.VMEM(queries.shape, bf16),
            pltpu.VMEM((S * QUERY_HEADS, HEAD_SIZE), jnp.float32),
            pltpu.VMEM((n, S, wo.shape[0]), bf16),
            pltpu.VMEM((SEQ_UNROLL, tokens, width), bf16),
            pltpu.VMEM((SEQ_UNROLL, tokens, width), bf16),
            pltpu.VMEM((2, S, width), bf16),
            pltpu.VMEM((S, width), jnp.float32),
            pltpu.VMEM((S, width), jnp.float32),
            pltpu.VMEM(pages, bf16),
            pltpu.VMEM(pages, bf16),
            pltpu.VMEM((S, 128), jnp.float32),
            pltpu.VMEM(hidden.shape, bf16),
            pltpu.VMEM(gain.shape, jnp.float32),
            dma((12,)),
            dma((2, n)), dma((2, n)), dma((n,)), dma((n,)),
            dma((n,)), dma((n,)), dma((n,)), dma((n,)),
            dma((2, 6, G)),
            dma((G, 2)), dma((G,)), dma((G, 2)), dma((G, 2, 2)),
        ],
        compiler_params=pltpu.CompilerParams(
            collective_id=0, has_side_effects=True, vmem_limit_bytes=63 * 1024 * 1024
        ),
    )(lengths, page_order, mig_pages, mig_dest, ids, weights, queries, fresh_keys, fresh_values,
      keys, values, hidden, gain, wo, wgu, wd)


def hand_out_kernel(a_ref, b_ref, c_ref, x_ref, y_ref, z_ref, sem):
    copies = [
        pltpu.make_async_copy(source, target, sem.at[i])
        for i, (source, target) in enumerate(((a_ref, x_ref), (b_ref, y_ref), (c_ref, z_ref)))
    ]
    for copy in copies:
        copy.start()
    for copy in copies:
        copy.wait()


def hand_out(*results):
    anywhere = pl.BlockSpec(memory_space=pl.ANY)
    return pl.pallas_call(
        hand_out_kernel,
        out_shape=tuple(jax.ShapeDtypeStruct(r.shape, r.dtype) for r in results),
        in_specs=[anywhere] * 3,
        out_specs=(anywhere,) * 3,
        scratch_shapes=[pltpu.SemaphoreType.DMA((3,))],
    )(*results)


def on_device(
    queries, fresh_token_keys, fresh_token_values, pooled_keys, pooled_values, lengths, page_order,
    hidden, out_weight, norm_gain, expert_ids, gate_weights, expert_gate_up, expert_down,
    mig_pages, mig_dest,
):
    n = lax.axis_size("ep")
    return hand_out(*layer(
        n, lengths, page_order, mig_pages, mig_dest.T, expert_ids.T, gate_weights.T, queries,
        fresh_token_keys, fresh_token_values, pooled_keys,
        pooled_values, hidden, norm_gain[None, :], out_weight,
        expert_gate_up.reshape(-1, PAGE_TOKENS, expert_gate_up.shape[2]), expert_down[0],
    ))


def solution(mesh):
    return jax.shard_map(
        on_device,
        mesh=mesh,
        in_specs=(
            P(("parts", "ep"), None),
            P(("parts", "ep"), None),
            P(("parts", "ep"), None),
            P(("parts", "ep"), None, None),
            P(("parts", "ep"), None, None),
            P(("parts", "ep"), None),
            P(("parts", "ep"), None),
            P(("parts", "ep"), None),
            P("ep", None),
            P(),
            P(("parts", "ep"), None),
            P(("parts", "ep"), None),
            P("ep", None, None),
            P("ep", None, None),
            P(("parts", "ep"), None),
            P(("parts", "ep"), None),
        ),
        out_specs=(
            P(("parts", "ep"), None),
            P(("parts", "ep"), None, None),
            P(("parts", "ep"), None, None),
        ),
        check_vma=False,
    )
```

```python
import functools
import math

import jax
import jax.numpy as jnp
from jax import lax
from jax.experimental import pallas as pl
from jax.experimental.pallas import tpu as pltpu
from jax.sharding import PartitionSpec as P

QUERY_HEADS = 64
KEY_VALUE_HEADS = 4
HEAD_SIZE = 128
PAGE_TOKENS = 16
MOST_SEQ_PAGES = 16
SEQ_UNROLL = 4
PLANE = 4
MESH = pl.DeviceIdType.MESH


def layer_kernel(
    n, len_ref, order_ref, mig_page_ref, mig_dest_ref, ids_ref, weights_ref,
    q_hbm, fk_hbm, fv_hbm, k_hbm, v_hbm, hidden_hbm, gain_hbm, wo_hbm, wgu_hbm, wd_hbm,
    out_ref, ak_ref, av_ref,
    wo, wgu, wd, heads, gates, part, crecv, yrecv, zrecv, rows, act, mid, acc,
    q_in, qs, attn_ref, ks, vs, fresh, fkf, fvf, mk_ref, mv_ref, gate_ref, hidden_ref, gain_ref,
    wsem, asend, arecv, gsend, grecv, ksend, krecv, vsend, vrecv, rs, nsz, nsy, nsc, nrecv,
):
    G = n // PLANE
    me = lax.axis_index("ep")
    g = lax.div(me, PLANE)
    lane = lax.rem(me, PLANE)
    b = lax.div(lane, 2)
    c = lax.rem(lane, 2)
    S = hidden_ref.shape[0]
    D = hidden_ref.shape[1]
    FFW = wd_hbm.shape[0]
    block_rows = PLANE * S

    def dev(gg, bb, cc):
        return {"ep": gg * PLANE + bb * 2 + cc}

    def remote(src, dst, send, recv, to):
        return pltpu.make_async_remote_copy(
            src_ref=src, dst_ref=dst, send_sem=send, recv_sem=recv, device_id=to,
            device_id_type=MESH,
        )

    pages = k_hbm.shape[0]
    width = KEY_VALUE_HEADS * HEAD_SIZE
    kpool = wgu.at[0:pages, :, 0:width]
    vpool = wgu.at[0:pages, :, width:2 * width]
    load_k = pltpu.make_async_copy(k_hbm, kpool, wsem.at[0])
    load_v = pltpu.make_async_copy(v_hbm, vpool, wsem.at[1])
    load_q = pltpu.make_async_copy(q_hbm, q_in, wsem.at[2])
    load_fk = pltpu.make_async_copy(fk_hbm, fresh.at[0], wsem.at[3])
    load_fv = pltpu.make_async_copy(fv_hbm, fresh.at[1], wsem.at[4])
    load_wo = pltpu.make_async_copy(wo_hbm, wo, wsem.at[5])
    load_wd = pltpu.make_async_copy(wd_hbm, wd, wsem.at[6])
    load_hidden = pltpu.make_async_copy(hidden_hbm, hidden_ref, wsem.at[7])
    load_gain = pltpu.make_async_copy(gain_hbm, gain_ref, wsem.at[8])
    load_wgu = pltpu.make_async_copy(wgu_hbm, wgu, wsem.at[9])
    own_k = pltpu.make_async_copy(mk_ref.at[me], ak_ref.at[me], wsem.at[10])
    own_v = pltpu.make_async_copy(mv_ref.at[me], av_ref.at[me], wsem.at[11])
    for load in (load_q, load_fk, load_fv, load_k, load_v, load_wo, load_wd, load_hidden,
                 load_gain):
        load.start()

    barrier = pltpu.get_barrier_semaphore()

    @pl.loop(1, n)
    def _(i):
        pl.semaphore_signal(
            barrier, inc=1, device_id={"ep": lax.rem(me + i, n)}, device_id_type=MESH
        )

    experts = lax.broadcasted_iota(jnp.int32, (128, S), 0)
    table = jnp.zeros((128, S), jnp.float32)
    for k in range(ids_ref.shape[0]):
        table = table + jnp.where(experts == ids_ref[k:k + 1, :], weights_ref[k:k + 1, :], 0.0)
    table = jnp.concatenate([table, jnp.zeros((128, 128 - S), jnp.float32)], axis=1)
    gate_ref[...] = table.T[0:S, :]
    gates[me] = gate_ref[...]

    def near(t):
        closest = jnp.minimum(g, G - 1 - g)
        away = lax.div(t + 1, 2)
        side = jnp.where(lax.rem(t, 2) == 1, g - away, g + away)
        rest = jnp.where(g + g <= G - 1, t, G - 1 - t)
        return jnp.where(t <= closest + closest, side, rest)

    def peer_of(k):
        plane = near(G - 1 - lax.div(k, PLANE))
        return plane * PLANE + lax.rem(lane + 1 + lax.rem(k, PLANE), PLANE)

    half_rows = S // 2

    def attn_copy(slot, peer, part_no):
        at = pl.ds(pl.multiple_of(part_no * half_rows, half_rows), half_rows)
        return remote(attn_ref.at[peer, at], heads.at[slot, at], asend.at[part_no, peer],
                      arecv.at[part_no, slot], {"ep": peer})

    def gate_copy(slot, peer):
        return remote(gate_ref, gates.at[slot], gsend.at[peer], grecv.at[slot], {"ep": peer})

    def key_copy(slot, peer):
        return remote(mk_ref.at[peer], ak_ref.at[slot], ksend.at[peer], krecv.at[slot],
                      {"ep": peer})

    def value_copy(slot, peer):
        return remote(mv_ref.at[peer], av_ref.at[slot], vsend.at[peer], vrecv.at[slot],
                      {"ep": peer})

    def stage_pages(dest):
        page, found = jnp.int32(0), jnp.int32(0)
        for i in range(mig_page_ref.shape[1]):
            same = mig_dest_ref[0, i] == dest
            page = jnp.where(same, mig_page_ref[0, i], page)
            found = jnp.where(same, 1, found)
        keep = jnp.full((PAGE_TOKENS, width), found, jnp.int32) == 1
        zero = jnp.zeros((PAGE_TOKENS, width), jnp.float32)
        for pool, staged in ((0, mk_ref), (width, mv_ref)):
            rows_of = wgu[page, :, pool:pool + width].astype(jnp.float32)
            staged[dest] = jnp.where(keep, rows_of, zero).astype(jnp.bfloat16)

    load_q.wait()
    load_fk.wait()
    load_fv.wait()
    for h in range(QUERY_HEADS):
        qs[pl.ds(h, S, stride=QUERY_HEADS), :] = q_in[
            :, h * HEAD_SIZE:(h + 1) * HEAD_SIZE
        ].astype(jnp.float32)
    fkf[...] = fresh[0].astype(jnp.float32)
    fvf[...] = fresh[1].astype(jnp.float32)

    load_k.wait()
    load_v.wait()
    stage_pages(me)
    own_k.start()
    own_v.start()
    pl.semaphore_wait(barrier, n - 1)

    @pl.loop(0, n - 1)
    def _(k):
        peer = peer_of(k)
        stage_pages(peer)
        key_copy(me, peer).start()
        value_copy(me, peer).start()
        gate_copy(me, peer).start()

    group = QUERY_HEADS // KEY_VALUE_HEADS
    tokens = MOST_SEQ_PAGES * PAGE_TOKENS
    score_scale = 1.0 / math.sqrt(HEAD_SIZE)
    row_head = lax.broadcasted_iota(jnp.int32, (QUERY_HEADS, width), 0) // group
    col_head = lax.broadcasted_iota(jnp.int32, (QUERY_HEADS, width), 1) // HEAD_SIZE
    diagonal = (row_head == col_head).astype(jnp.float32).astype(jnp.bfloat16)
    place = lax.broadcasted_iota(jnp.int32, (QUERY_HEADS, tokens), 1)

    def attend_some(part_no, i, start):
        first = part_no * half_rows + i * SEQ_UNROLL
        several = range(SEQ_UNROLL)
        spans, lengths, q_wides, scores, owns, probs, own_probs, results = ([] for _ in range(8))
        for u in several:
            s = first + u
            lengths.append(len_ref[0, s])
            for p in range(MOST_SEQ_PAGES):
                page = order_ref[0, jnp.minimum(start + p, pages - 1)]
                ks[u, p * PAGE_TOKENS:(p + 1) * PAGE_TOKENS, :] = wgu[page, :, 0:width]
                vs[u, p * PAGE_TOKENS:(p + 1) * PAGE_TOKENS, :] = wgu[page, :, width:2 * width]
            start = start + lax.div(lengths[u] + (PAGE_TOKENS - 1), PAGE_TOKENS)
            spans.append(pl.ds(pl.multiple_of(s * QUERY_HEADS, QUERY_HEADS), QUERY_HEADS))
            q = qs[spans[u], :].astype(jnp.bfloat16)
            q_wides.append(jnp.concatenate([q] * KEY_VALUE_HEADS, axis=1) * diagonal)
        for u in several:
            scores.append(lax.dot_general(
                q_wides[u], ks[u], (((1,), (1,)), ((), ())), preferred_element_type=jnp.float32
            ) * score_scale)
        for u in several:
            owns.append(jnp.sum(
                q_wides[u].astype(jnp.float32) * fkf[pl.ds(first + u, 1), :], axis=1,
                keepdims=True,
            ) * score_scale)
        for u in several:
            masked = jnp.where(place < lengths[u], scores[u], -1e30)
            highest = jnp.maximum(jnp.max(masked, axis=1, keepdims=True), owns[u])
            weights = jnp.exp(masked - highest)
            own_weight = jnp.exp(owns[u] - highest)
            inverse = 1.0 / (jnp.sum(weights, axis=1, keepdims=True) + own_weight)
            probs.append((weights * inverse).astype(jnp.bfloat16))
            own_probs.append((own_weight * inverse).astype(jnp.bfloat16).astype(jnp.float32))
        for u in several:
            mixed = jnp.dot(probs[u], vs[u], preferred_element_type=jnp.float32)
            fresh_value = fvf[pl.ds(first + u, 1), :]
            results.append(jnp.concatenate(
                [
                    mixed[h * group:(h + 1) * group, h * HEAD_SIZE:(h + 1) * HEAD_SIZE]
                    + own_probs[u][h * group:(h + 1) * group]
                    * fresh_value[:, h * HEAD_SIZE:(h + 1) * HEAD_SIZE]
                    for h in range(KEY_VALUE_HEADS)
                ],
                axis=0,
            ))
        for u in several:
            qs[spans[u], :] = results[u]
        return start

    some = half_rows // SEQ_UNROLL
    head_share = QUERY_HEADS // n

    def attend_half(part_no, start):
        start = lax.fori_loop(0, some, functools.partial(attend_some, part_no), start)
        at = pl.ds(pl.multiple_of(part_no * half_rows, half_rows), half_rows)
        first = part_no * (half_rows * QUERY_HEADS)
        for h in range(QUERY_HEADS):
            d, j = h // head_share, h % head_share
            attn_ref[d, at, j * HEAD_SIZE:(j + 1) * HEAD_SIZE] = qs[
                pl.ds(first + h, half_rows, stride=QUERY_HEADS), :
            ].astype(jnp.bfloat16)

        @pl.loop(0, n - 1)
        def _(k):
            attn_copy(me, peer_of(k), part_no).start()

        return start

    lax.fori_loop(0, 2, attend_half, jnp.int32(0))
    heads[me] = attn_ref[me]
    load_wgu.start()

    def c_copy(r, gi):
        return remote(part.at[gi, :, 1 - c], crecv.at[r, gi], rs.at[r, 0, gi], rs.at[r, 1, gi],
                      dev(g, b, 1 - c))

    def y_copy(r, gi):
        return remote(crecv.at[r, gi, 1 - b], yrecv.at[r, gi], rs.at[r, 2, gi], rs.at[r, 3, gi],
                      dev(g, 1 - b, c))

    def z_copy(r, gi, slot):
        return remote(yrecv.at[r, gi], zrecv.at[r, slot], rs.at[r, 4, gi], rs.at[r, 5, slot],
                      dev(gi, b, c))

    def core_stage(r, gi):
        c_copy(r, gi).wait_recv()
        for bb in range(2):
            crecv[r, gi, bb] = (
                part[gi, bb, c].astype(jnp.float32) + crecv[r, gi, bb].astype(jnp.float32)
            ).astype(jnp.bfloat16)
        y_copy(r, gi).start()

    def y_stage(r, gi):
        y_copy(r, gi).wait_recv()
        yrecv[r, gi] = (
            crecv[r, gi, b].astype(jnp.float32) + yrecv[r, gi].astype(jnp.float32)
        ).astype(jnp.bfloat16)

    def collect(r):
        acc[...] = yrecv[r, g].astype(jnp.float32)

        @pl.loop(1, G)
        def _(i):
            src = lax.rem(g + i, G)
            z_copy(r, g, src).wait_recv()
            acc[...] += zrecv[r, src].astype(jnp.float32)

    load_wo.wait()
    tile = 1024

    @pl.loop(0, G + 2)
    def _(t):
        @pl.when(t < G)
        def _():
            gi = near(G - 1 - t)
            for j in range(PLANE):
                src = gi * PLANE + j

                @pl.when(src != me)
                def _():
                    attn_copy(src, src, 0).wait_recv()
                    attn_copy(src, src, 1).wait_recv()

            left = heads[pl.ds(gi * PLANE, PLANE)].reshape(block_rows, heads.shape[2])
            for j in range(D // tile):
                part[gi, :, :, :, j * tile:(j + 1) * tile] = jnp.dot(
                    left, wo[:, j * tile:(j + 1) * tile], preferred_element_type=jnp.float32
                ).astype(jnp.bfloat16).reshape(2, 2, S, tile)
            c_copy(0, gi).start()

        @pl.when((t >= 1) & (t <= G))
        def _():
            core_stage(0, near(G - t))

        @pl.when(t >= 2)
        def _():
            gi = near(G + 1 - t)
            y_stage(0, gi)

            @pl.when(t <= G)
            def _():
                z_copy(0, gi, g).start()

    collect(0)
    load_hidden.wait()
    load_gain.wait()
    middle = (hidden_ref[...].astype(jnp.float32) + acc[...]).astype(jnp.bfloat16)
    mid[...] = middle
    middle = middle.astype(jnp.float32)
    scale = lax.rsqrt(jnp.mean(middle * middle, axis=1, keepdims=True) + 1e-06)
    rows[g, b, c] = (middle * scale * gain_ref[...]).astype(jnp.bfloat16)

    def row_copy(gg, bb, cc, send, to):
        slot = rows.at[gg, bb, cc]
        return remote(slot, slot, send, nrecv.at[gg, bb, cc], to)

    def rows_to_z(gg, step):
        return row_copy(gg, b, c, nsz.at[gg, (step + 1) // 2], dev(g + step, b, c))

    def pass_on(gg, act_on):
        @pl.when((gg <= g) & (g + 1 < G))
        def _():
            act_on(rows_to_z(gg, 1))

        @pl.when((gg >= g) & (g >= 1))
        def _():
            act_on(rows_to_z(gg, -1))

    def rows_to_y(gg):
        return row_copy(gg, b, c, nsy.at[gg], dev(g, 1 - b, c))

    def rows_to_core(gg, bb):
        return row_copy(gg, bb, c, nsc.at[gg, bb], dev(g, b, 1 - c))

    def arrival(gg, bb, cc):
        return row_copy(gg, bb, cc, nsy.at[gg], dev(g, b, 1 - c))

    rows_to_core(g, b).start()
    rows_to_y(g).start()

    pass_on(g, lambda copy: copy.start())

    @pl.loop(0, n - 1)
    def _(k):
        peer = peer_of(k)
        gate_copy(peer, peer).wait_recv()

    @pl.loop(0, G)
    def _(gi):
        c_copy(0, gi).wait_send()

    load_wgu.wait()
    load_wd.wait()
    half = 256

    def take_along_z(gi):
        arrival(gi, b, c).wait_recv()
        pass_on(gi, lambda copy: copy.start())
        rows_to_y(gi).start()
        rows_to_core(gi, b).start()

    def turn(t):
        return near(lax.rem(t + 1, G))

    @pl.loop(0, G + 2)
    def _(t):
        @pl.when((t == 0) & (G > 1))
        def _():
            take_along_z(near(1))

        @pl.when(t + 2 < G)
        def _():
            take_along_z(near(t + 2))

        @pl.when(t < G)
        def _():
            gi = turn(t)
            arrival(gi, 1 - b, c).wait_recv()
            rows_to_core(gi, 1 - b).start()
            arrival(gi, b, 1 - c).wait_recv()
            arrival(gi, 1 - b, 1 - c).wait_recv()

            @pl.loop(0, FFW // half)
            def _(j):
                left = rows[gi].reshape(block_rows, D)
                at = pl.multiple_of(j * half, half)
                gate = jnp.dot(left, wgu[:, :, pl.ds(at, half)].reshape(D, half),
                               preferred_element_type=jnp.float32)
                up = jnp.dot(left, wgu[:, :, pl.ds(FFW + at, half)].reshape(D, half),
                             preferred_element_type=jnp.float32)
                act[:, pl.ds(at, half)] = (gate * jax.nn.sigmoid(gate) * up).astype(jnp.bfloat16)

            table = gates[pl.ds(gi * PLANE, PLANE)].reshape(block_rows, gates.shape[2])
            column = lax.broadcasted_iota(jnp.int32, table.shape, 1)
            chosen = jnp.sum(jnp.where(column == me, table, 0.0), axis=1, keepdims=True)
            for j in range(D // tile):
                y = jnp.dot(act[...], wd[:, j * tile:(j + 1) * tile],
                            preferred_element_type=jnp.float32)
                y = y.astype(jnp.bfloat16).astype(jnp.float32) * chosen
                part[gi, :, :, :, j * tile:(j + 1) * tile] = y.astype(jnp.bfloat16).reshape(
                    2, 2, S, tile
                )
            c_copy(1, gi).start()

        @pl.when((t >= 1) & (t <= G))
        def _():
            core_stage(1, turn(t - 1))

        @pl.when(t >= 2)
        def _():
            gi = turn(t - 2)
            y_stage(1, gi)

            @pl.when(t <= G)
            def _():
                z_copy(1, gi, g).start()

    collect(1)
    out_ref[...] = (mid[...].astype(jnp.float32) + acc[...]).astype(jnp.bfloat16)

    own_k.wait()
    own_v.wait()

    @pl.loop(0, n - 1)
    def _(k):
        peer = peer_of(k)
        attn_copy(me, peer, 0).wait_send()
        attn_copy(me, peer, 1).wait_send()
        gate_copy(me, peer).wait_send()
        key_copy(me, peer).wait_send()
        value_copy(me, peer).wait_send()
        key_copy(peer, peer).wait_recv()
        value_copy(peer, peer).wait_recv()

    @pl.loop(0, G)
    def _(gi):
        c_copy(1, gi).wait_send()
        rows_to_y(gi).wait_send()
        rows_to_core(gi, 0).wait_send()
        rows_to_core(gi, 1).wait_send()
        pass_on(gi, lambda copy: copy.wait_send())
        for r in range(2):
            y_copy(r, gi).wait_send()

    @pl.loop(1, G)
    def _(i):
        gi = lax.rem(g + i, G)
        for r in range(2):
            z_copy(r, gi, g).wait_send()


def layer(n, lengths, page_order, mig_pages, mig_dest, ids, weights, queries, fresh_keys,
          fresh_values, keys, values, hidden, gain, wo, wgu, wd):
    G = n // PLANE
    S, D = hidden.shape
    FFW = wd.shape[0]
    width = KEY_VALUE_HEADS * HEAD_SIZE
    tokens = MOST_SEQ_PAGES * PAGE_TOKENS
    pages = (n, PAGE_TOKENS, width)
    smem = pl.BlockSpec(memory_space=pltpu.SMEM)
    vmem = pl.BlockSpec(memory_space=pltpu.VMEM)
    anywhere = pl.BlockSpec(memory_space=pl.ANY)
    bf16 = jnp.bfloat16
    dma = pltpu.SemaphoreType.DMA
    return pl.pallas_call(
        functools.partial(layer_kernel, n),
        out_shape=(
            jax.ShapeDtypeStruct(hidden.shape, bf16),
            jax.ShapeDtypeStruct(pages, bf16),
            jax.ShapeDtypeStruct(pages, bf16),
        ),
        in_specs=[smem] * 4 + [vmem] * 2 + [anywhere] * 10,
        out_specs=(vmem, anywhere, anywhere),
        scratch_shapes=[
            pltpu.VMEM(wo.shape, bf16),
            pltpu.VMEM(wgu.shape, bf16),
            pltpu.VMEM(wd.shape, bf16),
            pltpu.VMEM((n, S, wo.shape[0]), bf16),
            pltpu.VMEM((n, S, 128), jnp.float32),
            pltpu.VMEM((G, 2, 2, S, D), bf16),
            pltpu.VMEM((2, G, 2, S, D), bf16),
            pltpu.VMEM((2, G, S, D), bf16),
            pltpu.VMEM((2, G, S, D), bf16),
            pltpu.VMEM((G, 2, 2, S, D), bf16),
            pltpu.VMEM((PLANE * S, FFW), bf16),
            pltpu.VMEM((S, D), bf16),
            pltpu.VMEM((S, D), jnp.float32),
            pltpu.VMEM(queries.shape, bf16),
            pltpu.VMEM((S * QUERY_HEADS, HEAD_SIZE), jnp.float32),
            pltpu.VMEM((n, S, wo.shape[0]), bf16),
            pltpu.VMEM((SEQ_UNROLL, tokens, width), bf16),
            pltpu.VMEM((SEQ_UNROLL, tokens, width), bf16),
            pltpu.VMEM((2, S, width), bf16),
            pltpu.VMEM((S, width), jnp.float32),
            pltpu.VMEM((S, width), jnp.float32),
            pltpu.VMEM(pages, bf16),
            pltpu.VMEM(pages, bf16),
            pltpu.VMEM((S, 128), jnp.float32),
            pltpu.VMEM(hidden.shape, bf16),
            pltpu.VMEM(gain.shape, jnp.float32),
            dma((12,)),
            dma((2, n)), dma((2, n)), dma((n,)), dma((n,)),
            dma((n,)), dma((n,)), dma((n,)), dma((n,)),
            dma((2, 6, G)),
            dma((G, 2)), dma((G,)), dma((G, 2)), dma((G, 2, 2)),
        ],
        compiler_params=pltpu.CompilerParams(
            collective_id=0, has_side_effects=True, vmem_limit_bytes=63 * 1024 * 1024
        ),
    )(lengths, page_order, mig_pages, mig_dest, ids, weights, queries, fresh_keys, fresh_values,
      keys, values, hidden, gain, wo, wgu, wd)


def hand_out_kernel(a_ref, b_ref, c_ref, x_ref, y_ref, z_ref, a_held, b_held, c_held, sem):
    moves = (
        (a_ref, a_held, x_ref), (b_ref, b_held, y_ref), (c_ref, c_held, z_ref)
    )
    loads = [pltpu.make_async_copy(s, h, sem.at[0, i]) for i, (s, h, _) in enumerate(moves)]
    stores = [pltpu.make_async_copy(h, t, sem.at[1, i]) for i, (_, h, t) in enumerate(moves)]
    for load in loads:
        load.start()
    for load, store in zip(loads, stores):
        load.wait()
        store.start()
    for store in stores:
        store.wait()


def hand_out(*results):
    anywhere = pl.BlockSpec(memory_space=pl.ANY)
    return pl.pallas_call(
        hand_out_kernel,
        out_shape=tuple(jax.ShapeDtypeStruct(r.shape, r.dtype) for r in results),
        in_specs=[anywhere] * 3,
        out_specs=(anywhere,) * 3,
        scratch_shapes=[pltpu.VMEM(r.shape, r.dtype) for r in results]
        + [pltpu.SemaphoreType.DMA((2, 3))],
    )(*results)


def on_device(
    queries, fresh_token_keys, fresh_token_values, pooled_keys, pooled_values, lengths, page_order,
    hidden, out_weight, norm_gain, expert_ids, gate_weights, expert_gate_up, expert_down,
    mig_pages, mig_dest,
):
    n = lax.axis_size("ep")
    return hand_out(*layer(
        n, lengths, page_order, mig_pages, mig_dest.T, expert_ids.T, gate_weights.T, queries,
        fresh_token_keys, fresh_token_values, pooled_keys,
        pooled_values, hidden, norm_gain[None, :], out_weight,
        expert_gate_up.reshape(-1, PAGE_TOKENS, expert_gate_up.shape[2]), expert_down[0],
    ))


def solution(mesh):
    return jax.shard_map(
        on_device,
        mesh=mesh,
        in_specs=(
            P(("parts", "ep"), None),
            P(("parts", "ep"), None),
            P(("parts", "ep"), None),
            P(("parts", "ep"), None, None),
            P(("parts", "ep"), None, None),
            P(("parts", "ep"), None),
            P(("parts", "ep"), None),
            P(("parts", "ep"), None),
            P("ep", None),
            P(),
            P(("parts", "ep"), None),
            P(("parts", "ep"), None),
            P("ep", None, None),
            P("ep", None, None),
            P(("parts", "ep"), None),
            P(("parts", "ep"), None),
        ),
        out_specs=(
            P(("parts", "ep"), None),
            P(("parts", "ep"), None, None),
            P(("parts", "ep"), None, None),
        ),
        check_vma=False,
    )
```

```python
import functools
import math

import jax
import jax.numpy as jnp
from jax import lax
from jax.experimental import pallas as pl
from jax.experimental.pallas import tpu as pltpu
from jax.sharding import PartitionSpec as P

QUERY_HEADS = 64
KEY_VALUE_HEADS = 4
HEAD_SIZE = 128
PAGE_TOKENS = 16
MOST_SEQ_PAGES = 16
SEQ_UNROLL = 4
PLANE = 4
MESH = pl.DeviceIdType.MESH


def layer_kernel(
    n, len_ref, order_ref, mig_page_ref, mig_dest_ref, ids_ref, weights_ref,
    q_hbm, fk_hbm, fv_hbm, k_hbm, v_hbm, hidden_hbm, gain_hbm, wo_hbm, wgu_hbm, wd_hbm,
    out_ref, ak_ref, av_ref,
    wo, wgu, wd, heads, gates, part, crecv, yrecv, zrecv, rows, act, mid, acc,
    q_in, qs, attn_ref, ks, vs, fresh, fkf, fvf, mk_ref, mv_ref, gate_ref, hidden_ref, gain_ref,
    wsem, asend, arecv, gsend, grecv, ksend, krecv, vsend, vrecv, rs, nsz, nsy, nsc, nrecv,
):
    G = n // PLANE
    me = lax.axis_index("ep")
    g = lax.div(me, PLANE)
    lane = lax.rem(me, PLANE)
    b = lax.div(lane, 2)
    c = lax.rem(lane, 2)
    S = hidden_ref.shape[0]
    D = hidden_ref.shape[1]
    FFW = wd_hbm.shape[0]
    block_rows = PLANE * S

    def dev(gg, bb, cc):
        return {"ep": gg * PLANE + bb * 2 + cc}

    def remote(src, dst, send, recv, to):
        return pltpu.make_async_remote_copy(
            src_ref=src, dst_ref=dst, send_sem=send, recv_sem=recv, device_id=to,
            device_id_type=MESH,
        )

    pages = k_hbm.shape[0]
    width = KEY_VALUE_HEADS * HEAD_SIZE
    kpool = wgu.at[0:pages, :, 0:width]
    vpool = wgu.at[0:pages, :, width:2 * width]
    load_k = pltpu.make_async_copy(k_hbm, kpool, wsem.at[0])
    load_v = pltpu.make_async_copy(v_hbm, vpool, wsem.at[1])
    load_q = pltpu.make_async_copy(q_hbm, q_in, wsem.at[2])
    load_fk = pltpu.make_async_copy(fk_hbm, fresh.at[0], wsem.at[3])
    load_fv = pltpu.make_async_copy(fv_hbm, fresh.at[1], wsem.at[4])
    load_wo = pltpu.make_async_copy(wo_hbm, wo, wsem.at[5])
    load_wd = pltpu.make_async_copy(wd_hbm, wd, wsem.at[6])
    load_hidden = pltpu.make_async_copy(hidden_hbm, hidden_ref, wsem.at[7])
    load_gain = pltpu.make_async_copy(gain_hbm, gain_ref, wsem.at[8])
    load_wgu = pltpu.make_async_copy(wgu_hbm, wgu, wsem.at[9])
    own_k = pltpu.make_async_copy(mk_ref.at[me], ak_ref.at[me], wsem.at[10])
    own_v = pltpu.make_async_copy(mv_ref.at[me], av_ref.at[me], wsem.at[11])
    for load in (load_q, load_fk, load_fv, load_k, load_v, load_wo, load_wd, load_hidden,
                 load_gain):
        load.start()

    barrier = pltpu.get_barrier_semaphore()

    @pl.loop(1, n)
    def _(i):
        pl.semaphore_signal(
            barrier, inc=1, device_id={"ep": lax.rem(me + i, n)}, device_id_type=MESH
        )

    experts = lax.broadcasted_iota(jnp.int32, (128, S), 0)
    table = jnp.zeros((128, S), jnp.float32)
    for k in range(ids_ref.shape[0]):
        table = table + jnp.where(experts == ids_ref[k:k + 1, :], weights_ref[k:k + 1, :], 0.0)
    table = jnp.concatenate([table, jnp.zeros((128, 128 - S), jnp.float32)], axis=1)
    gate_ref[...] = table.T[0:S, :]
    gates[me] = gate_ref[...]

    def near(t):
        closest = jnp.minimum(g, G - 1 - g)
        away = lax.div(t + 1, 2)
        side = jnp.where(lax.rem(t, 2) == 1, g - away, g + away)
        rest = jnp.where(g + g <= G - 1, t, G - 1 - t)
        return jnp.where(t <= closest + closest, side, rest)

    def peer_of(k):
        plane = near(G - 1 - lax.div(k, PLANE))
        return plane * PLANE + lax.rem(lane + 1 + lax.rem(k, PLANE), PLANE)

    half_rows = S // 2

    def attn_copy(slot, peer, part_no):
        at = pl.ds(pl.multiple_of(part_no * half_rows, half_rows), half_rows)
        return remote(attn_ref.at[peer, at], heads.at[slot, at], asend.at[part_no, peer],
                      arecv.at[part_no, slot], {"ep": peer})

    def gate_copy(slot, peer):
        return remote(gate_ref, gates.at[slot], gsend.at[peer], grecv.at[slot], {"ep": peer})

    def key_copy(slot, peer):
        return remote(mk_ref.at[peer], ak_ref.at[slot], ksend.at[peer], krecv.at[slot],
                      {"ep": peer})

    def value_copy(slot, peer):
        return remote(mv_ref.at[peer], av_ref.at[slot], vsend.at[peer], vrecv.at[slot],
                      {"ep": peer})

    def stage_pages(dest):
        page, found = jnp.int32(0), jnp.int32(0)
        for i in range(mig_page_ref.shape[1]):
            same = mig_dest_ref[0, i] == dest
            page = jnp.where(same, mig_page_ref[0, i], page)
            found = jnp.where(same, 1, found)
        keep = jnp.full((PAGE_TOKENS, width), found, jnp.int32) == 1
        zero = jnp.zeros((PAGE_TOKENS, width), jnp.float32)
        for pool, staged in ((0, mk_ref), (width, mv_ref)):
            rows_of = wgu[page, :, pool:pool + width].astype(jnp.float32)
            staged[dest] = jnp.where(keep, rows_of, zero).astype(jnp.bfloat16)

    load_q.wait()
    load_fk.wait()
    load_fv.wait()
    for h in range(QUERY_HEADS):
        qs[pl.ds(h, S, stride=QUERY_HEADS), :] = q_in[
            :, h * HEAD_SIZE:(h + 1) * HEAD_SIZE
        ].astype(jnp.float32)
    fkf[...] = fresh[0].astype(jnp.float32)
    fvf[...] = fresh[1].astype(jnp.float32)

    load_k.wait()
    load_v.wait()
    stage_pages(me)
    own_k.start()
    own_v.start()
    pl.semaphore_wait(barrier, n - 1)

    @pl.loop(0, n - 1)
    def _(k):
        peer = peer_of(k)
        stage_pages(peer)
        key_copy(me, peer).start()
        value_copy(me, peer).start()
        gate_copy(me, peer).start()

    group = QUERY_HEADS // KEY_VALUE_HEADS
    tokens = MOST_SEQ_PAGES * PAGE_TOKENS
    score_scale = 1.0 / math.sqrt(HEAD_SIZE)
    row_head = lax.broadcasted_iota(jnp.int32, (QUERY_HEADS, width), 0) // group
    col_head = lax.broadcasted_iota(jnp.int32, (QUERY_HEADS, width), 1) // HEAD_SIZE
    diagonal = (row_head == col_head).astype(jnp.float32).astype(jnp.bfloat16)
    place = lax.broadcasted_iota(jnp.int32, (QUERY_HEADS, tokens), 1)

    def attend_some(part_no, i, start):
        first = part_no * half_rows + i * SEQ_UNROLL
        several = range(SEQ_UNROLL)
        spans, lengths, q_wides, scores, owns, probs, own_probs, results = ([] for _ in range(8))
        for u in several:
            s = first + u
            lengths.append(len_ref[0, s])
            for p in range(MOST_SEQ_PAGES):
                page = order_ref[0, jnp.minimum(start + p, pages - 1)]
                ks[u, p * PAGE_TOKENS:(p + 1) * PAGE_TOKENS, :] = wgu[page, :, 0:width]
                vs[u, p * PAGE_TOKENS:(p + 1) * PAGE_TOKENS, :] = wgu[page, :, width:2 * width]
            start = start + lax.div(lengths[u] + (PAGE_TOKENS - 1), PAGE_TOKENS)
            spans.append(pl.ds(pl.multiple_of(s * QUERY_HEADS, QUERY_HEADS), QUERY_HEADS))
            q = qs[spans[u], :].astype(jnp.bfloat16)
            q_wides.append(jnp.concatenate([q] * KEY_VALUE_HEADS, axis=1) * diagonal)
        for u in several:
            scores.append(lax.dot_general(
                q_wides[u], ks[u], (((1,), (1,)), ((), ())), preferred_element_type=jnp.float32
            ) * score_scale)
        for u in several:
            owns.append(jnp.sum(
                q_wides[u].astype(jnp.float32) * fkf[pl.ds(first + u, 1), :], axis=1,
                keepdims=True,
            ) * score_scale)
        for u in several:
            masked = jnp.where(place < lengths[u], scores[u], -1e30)
            highest = jnp.maximum(jnp.max(masked, axis=1, keepdims=True), owns[u])
            weights = jnp.exp(masked - highest)
            own_weight = jnp.exp(owns[u] - highest)
            inverse = 1.0 / (jnp.sum(weights, axis=1, keepdims=True) + own_weight)
            probs.append((weights * inverse).astype(jnp.bfloat16))
            own_probs.append((own_weight * inverse).astype(jnp.bfloat16).astype(jnp.float32))
        for u in several:
            mixed = jnp.dot(probs[u], vs[u], preferred_element_type=jnp.float32)
            fresh_value = fvf[pl.ds(first + u, 1), :]
            results.append(jnp.concatenate(
                [
                    mixed[h * group:(h + 1) * group, h * HEAD_SIZE:(h + 1) * HEAD_SIZE]
                    + own_probs[u][h * group:(h + 1) * group]
                    * fresh_value[:, h * HEAD_SIZE:(h + 1) * HEAD_SIZE]
                    for h in range(KEY_VALUE_HEADS)
                ],
                axis=0,
            ))
        for u in several:
            qs[spans[u], :] = results[u]
        return start

    some = half_rows // SEQ_UNROLL
    head_share = QUERY_HEADS // n

    def attend_half(part_no, start):
        start = lax.fori_loop(0, some, functools.partial(attend_some, part_no), start)
        at = pl.ds(pl.multiple_of(part_no * half_rows, half_rows), half_rows)
        first = part_no * (half_rows * QUERY_HEADS)
        for h in range(QUERY_HEADS):
            d, j = h // head_share, h % head_share
            attn_ref[d, at, j * HEAD_SIZE:(j + 1) * HEAD_SIZE] = qs[
                pl.ds(first + h, half_rows, stride=QUERY_HEADS), :
            ].astype(jnp.bfloat16)

        @pl.loop(0, n - 1)
        def _(k):
            attn_copy(me, peer_of(k), part_no).start()

        return start

    lax.fori_loop(0, 2, attend_half, jnp.int32(0))
    heads[me] = attn_ref[me]
    load_wgu.start()

    def c_copy(r, gi):
        return remote(part.at[gi, :, 1 - c], crecv.at[r, gi], rs.at[r, 0, gi], rs.at[r, 1, gi],
                      dev(g, b, 1 - c))

    def y_copy(r, gi):
        return remote(crecv.at[r, gi, 1 - b], yrecv.at[r, gi], rs.at[r, 2, gi], rs.at[r, 3, gi],
                      dev(g, 1 - b, c))

    def z_copy(r, gi, slot):
        return remote(yrecv.at[r, gi], zrecv.at[r, slot], rs.at[r, 4, gi], rs.at[r, 5, slot],
                      dev(gi, b, c))

    def core_stage(r, gi):
        c_copy(r, gi).wait_recv()
        for bb in range(2):
            crecv[r, gi, bb] = (
                part[gi, bb, c].astype(jnp.float32) + crecv[r, gi, bb].astype(jnp.float32)
            ).astype(jnp.bfloat16)
        y_copy(r, gi).start()

    def y_stage(r, gi):
        y_copy(r, gi).wait_recv()
        yrecv[r, gi] = (
            crecv[r, gi, b].astype(jnp.float32) + yrecv[r, gi].astype(jnp.float32)
        ).astype(jnp.bfloat16)

    def line_copy(gi):
        step = jnp.where(gi > g, 1, -1)
        slot = jnp.where((step < 0) & (g + step == gi), G, gi)
        return remote(yrecv.at[0, gi], zrecv.at[0, slot], rs.at[0, 4, gi], rs.at[0, 5, slot],
                      dev(g + step, b, c))

    def line_arrival(slot):
        return remote(zrecv.at[0, slot], zrecv.at[0, slot], rs.at[0, 4, 0], rs.at[0, 5, slot],
                      dev(g, b, 1 - c))

    def starts_line(gi):
        return ((gi > g) & (g == 0)) | ((gi < g) & (g == G - 1))

    def line_stage(gi):
        line_arrival(gi).wait_recv()
        yrecv[0, gi] = (
            yrecv[0, gi].astype(jnp.float32) + zrecv[0, gi].astype(jnp.float32)
        ).astype(jnp.bfloat16)
        line_copy(gi).start()

    def collect_line():
        acc[...] = yrecv[0, g].astype(jnp.float32)
        for slot, there in ((g, g > 0), (G, g < G - 1)):
            @pl.when(there)
            def _():
                line_arrival(slot).wait_recv()
                acc[...] += zrecv[0, slot].astype(jnp.float32)

    def collect(r):
        acc[...] = yrecv[r, g].astype(jnp.float32)

        @pl.loop(1, G)
        def _(i):
            src = lax.rem(g + i, G)
            z_copy(r, g, src).wait_recv()
            acc[...] += zrecv[r, src].astype(jnp.float32)

    load_wo.wait()
    tile = 1024

    @pl.loop(0, G + 2)
    def _(t):
        @pl.when(t < G)
        def _():
            gi = near(G - 1 - t)
            for j in range(PLANE):
                src = gi * PLANE + j

                @pl.when(src != me)
                def _():
                    attn_copy(src, src, 0).wait_recv()
                    attn_copy(src, src, 1).wait_recv()

            left = heads[pl.ds(gi * PLANE, PLANE)].reshape(block_rows, heads.shape[2])
            for j in range(D // tile):
                part[gi, :, :, :, j * tile:(j + 1) * tile] = jnp.dot(
                    left, wo[:, j * tile:(j + 1) * tile], preferred_element_type=jnp.float32
                ).astype(jnp.bfloat16).reshape(2, 2, S, tile)
            c_copy(0, gi).start()

        @pl.when((t >= 1) & (t <= G))
        def _():
            core_stage(0, near(G - t))

        @pl.when(t >= 3)
        def _():
            gi = near(G + 2 - t)

            @pl.when(jnp.logical_not(starts_line(gi)))
            def _():
                line_stage(gi)

        @pl.when(t >= 2)
        def _():
            gi = near(G + 1 - t)
            y_stage(0, gi)

            @pl.when(starts_line(gi))
            def _():
                line_copy(gi).start()

    collect_line()
    load_hidden.wait()
    load_gain.wait()
    middle = (hidden_ref[...].astype(jnp.float32) + acc[...]).astype(jnp.bfloat16)
    mid[...] = middle
    middle = middle.astype(jnp.float32)
    scale = lax.rsqrt(jnp.mean(middle * middle, axis=1, keepdims=True) + 1e-06)
    rows[g, b, c] = (middle * scale * gain_ref[...]).astype(jnp.bfloat16)

    def row_copy(gg, bb, cc, send, to):
        slot = rows.at[gg, bb, cc]
        return remote(slot, slot, send, nrecv.at[gg, bb, cc], to)

    def rows_to_z(gg, step):
        return row_copy(gg, b, c, nsz.at[gg, (step + 1) // 2], dev(g + step, b, c))

    def pass_on(gg, act_on):
        @pl.when((gg <= g) & (g + 1 < G))
        def _():
            act_on(rows_to_z(gg, 1))

        @pl.when((gg >= g) & (g >= 1))
        def _():
            act_on(rows_to_z(gg, -1))

    def rows_to_y(gg):
        return row_copy(gg, b, c, nsy.at[gg], dev(g, 1 - b, c))

    def rows_to_core(gg, bb):
        return row_copy(gg, bb, c, nsc.at[gg, bb], dev(g, b, 1 - c))

    def arrival(gg, bb, cc):
        return row_copy(gg, bb, cc, nsy.at[gg], dev(g, b, 1 - c))

    rows_to_core(g, b).start()
    rows_to_y(g).start()

    pass_on(g, lambda copy: copy.start())

    @pl.loop(0, n - 1)
    def _(k):
        peer = peer_of(k)
        gate_copy(peer, peer).wait_recv()

    @pl.loop(0, G)
    def _(gi):
        c_copy(0, gi).wait_send()

    load_wgu.wait()
    load_wd.wait()
    half = 256

    def take_along_z(gi):
        arrival(gi, b, c).wait_recv()
        pass_on(gi, lambda copy: copy.start())
        rows_to_y(gi).start()
        rows_to_core(gi, b).start()

    def turn(t):
        return near(lax.rem(t + 1, G))

    @pl.loop(0, G + 2)
    def _(t):
        @pl.when((t == 0) & (G > 1))
        def _():
            take_along_z(near(1))

        @pl.when(t + 2 < G)
        def _():
            take_along_z(near(t + 2))

        @pl.when(t < G)
        def _():
            gi = turn(t)
            arrival(gi, 1 - b, c).wait_recv()
            rows_to_core(gi, 1 - b).start()
            arrival(gi, b, 1 - c).wait_recv()
            arrival(gi, 1 - b, 1 - c).wait_recv()

            @pl.loop(0, FFW // half)
            def _(j):
                left = rows[gi].reshape(block_rows, D)
                at = pl.multiple_of(j * half, half)
                gate = jnp.dot(left, wgu[:, :, pl.ds(at, half)].reshape(D, half),
                               preferred_element_type=jnp.float32)
                up = jnp.dot(left, wgu[:, :, pl.ds(FFW + at, half)].reshape(D, half),
                             preferred_element_type=jnp.float32)
                act[:, pl.ds(at, half)] = (gate * jax.nn.sigmoid(gate) * up).astype(jnp.bfloat16)

            table = gates[pl.ds(gi * PLANE, PLANE)].reshape(block_rows, gates.shape[2])
            column = lax.broadcasted_iota(jnp.int32, table.shape, 1)
            chosen = jnp.sum(jnp.where(column == me, table, 0.0), axis=1, keepdims=True)
            for j in range(D // tile):
                y = jnp.dot(act[...], wd[:, j * tile:(j + 1) * tile],
                            preferred_element_type=jnp.float32)
                y = y.astype(jnp.bfloat16).astype(jnp.float32) * chosen
                part[gi, :, :, :, j * tile:(j + 1) * tile] = y.astype(jnp.bfloat16).reshape(
                    2, 2, S, tile
                )
            c_copy(1, gi).start()

        @pl.when((t >= 1) & (t <= G))
        def _():
            core_stage(1, turn(t - 1))

        @pl.when(t >= 2)
        def _():
            gi = turn(t - 2)
            y_stage(1, gi)

            @pl.when(t <= G)
            def _():
                z_copy(1, gi, g).start()

    collect(1)
    out_ref[...] = (mid[...].astype(jnp.float32) + acc[...]).astype(jnp.bfloat16)

    own_k.wait()
    own_v.wait()

    @pl.loop(0, n - 1)
    def _(k):
        peer = peer_of(k)
        attn_copy(me, peer, 0).wait_send()
        attn_copy(me, peer, 1).wait_send()
        gate_copy(me, peer).wait_send()
        key_copy(me, peer).wait_send()
        value_copy(me, peer).wait_send()
        key_copy(peer, peer).wait_recv()
        value_copy(peer, peer).wait_recv()

    @pl.loop(0, G)
    def _(gi):
        c_copy(1, gi).wait_send()
        rows_to_y(gi).wait_send()
        rows_to_core(gi, 0).wait_send()
        rows_to_core(gi, 1).wait_send()
        pass_on(gi, lambda copy: copy.wait_send())
        for r in range(2):
            y_copy(r, gi).wait_send()

    @pl.loop(1, G)
    def _(i):
        gi = lax.rem(g + i, G)
        line_copy(gi).wait_send()
        z_copy(1, gi, g).wait_send()


def layer(n, lengths, page_order, mig_pages, mig_dest, ids, weights, queries, fresh_keys,
          fresh_values, keys, values, hidden, gain, wo, wgu, wd):
    G = n // PLANE
    S, D = hidden.shape
    FFW = wd.shape[0]
    width = KEY_VALUE_HEADS * HEAD_SIZE
    tokens = MOST_SEQ_PAGES * PAGE_TOKENS
    pages = (n, PAGE_TOKENS, width)
    smem = pl.BlockSpec(memory_space=pltpu.SMEM)
    vmem = pl.BlockSpec(memory_space=pltpu.VMEM)
    anywhere = pl.BlockSpec(memory_space=pl.ANY)
    bf16 = jnp.bfloat16
    dma = pltpu.SemaphoreType.DMA
    return pl.pallas_call(
        functools.partial(layer_kernel, n),
        out_shape=(
            jax.ShapeDtypeStruct(hidden.shape, bf16),
            jax.ShapeDtypeStruct(pages, bf16),
            jax.ShapeDtypeStruct(pages, bf16),
        ),
        in_specs=[smem] * 4 + [vmem] * 2 + [anywhere] * 10,
        out_specs=(vmem, anywhere, anywhere),
        scratch_shapes=[
            pltpu.VMEM(wo.shape, bf16),
            pltpu.VMEM(wgu.shape, bf16),
            pltpu.VMEM(wd.shape, bf16),
            pltpu.VMEM((n, S, wo.shape[0]), bf16),
            pltpu.VMEM((n, S, 128), jnp.float32),
            pltpu.VMEM((G, 2, 2, S, D), bf16),
            pltpu.VMEM((2, G, 2, S, D), bf16),
            pltpu.VMEM((2, G, S, D), bf16),
            pltpu.VMEM((2, G + 1, S, D), bf16),
            pltpu.VMEM((G, 2, 2, S, D), bf16),
            pltpu.VMEM((PLANE * S, FFW), bf16),
            pltpu.VMEM((S, D), bf16),
            pltpu.VMEM((S, D), jnp.float32),
            pltpu.VMEM(queries.shape, bf16),
            pltpu.VMEM((S * QUERY_HEADS, HEAD_SIZE), jnp.float32),
            pltpu.VMEM((n, S, wo.shape[0]), bf16),
            pltpu.VMEM((SEQ_UNROLL, tokens, width), bf16),
            pltpu.VMEM((SEQ_UNROLL, tokens, width), bf16),
            pltpu.VMEM((2, S, width), bf16),
            pltpu.VMEM((S, width), jnp.float32),
            pltpu.VMEM((S, width), jnp.float32),
            pltpu.VMEM(pages, bf16),
            pltpu.VMEM(pages, bf16),
            pltpu.VMEM((S, 128), jnp.float32),
            pltpu.VMEM(hidden.shape, bf16),
            pltpu.VMEM(gain.shape, jnp.float32),
            dma((12,)),
            dma((2, n)), dma((2, n)), dma((n,)), dma((n,)),
            dma((n,)), dma((n,)), dma((n,)), dma((n,)),
            dma((2, 6, G + 1)),
            dma((G, 2)), dma((G,)), dma((G, 2)), dma((G, 2, 2)),
        ],
        compiler_params=pltpu.CompilerParams(
            collective_id=0, has_side_effects=True, vmem_limit_bytes=63 * 1024 * 1024
        ),
    )(lengths, page_order, mig_pages, mig_dest, ids, weights, queries, fresh_keys, fresh_values,
      keys, values, hidden, gain, wo, wgu, wd)


def hand_out_kernel(a_ref, b_ref, c_ref, x_ref, y_ref, z_ref, a_held, b_held, c_held, sem):
    moves = (
        (a_ref, a_held, x_ref), (b_ref, b_held, y_ref), (c_ref, c_held, z_ref)
    )
    loads = [pltpu.make_async_copy(s, h, sem.at[0, i]) for i, (s, h, _) in enumerate(moves)]
    stores = [pltpu.make_async_copy(h, t, sem.at[1, i]) for i, (_, h, t) in enumerate(moves)]
    for load in loads:
        load.start()
    for load, store in zip(loads, stores):
        load.wait()
        store.start()
    for store in stores:
        store.wait()


def hand_out(*results):
    anywhere = pl.BlockSpec(memory_space=pl.ANY)
    return pl.pallas_call(
        hand_out_kernel,
        out_shape=tuple(jax.ShapeDtypeStruct(r.shape, r.dtype) for r in results),
        in_specs=[anywhere] * 3,
        out_specs=(anywhere,) * 3,
        scratch_shapes=[pltpu.VMEM(r.shape, r.dtype) for r in results]
        + [pltpu.SemaphoreType.DMA((2, 3))],
    )(*results)


def on_device(
    queries, fresh_token_keys, fresh_token_values, pooled_keys, pooled_values, lengths, page_order,
    hidden, out_weight, norm_gain, expert_ids, gate_weights, expert_gate_up, expert_down,
    mig_pages, mig_dest,
):
    n = lax.axis_size("ep")
    return hand_out(*layer(
        n, lengths, page_order, mig_pages, mig_dest.T, expert_ids.T, gate_weights.T, queries,
        fresh_token_keys, fresh_token_values, pooled_keys,
        pooled_values, hidden, norm_gain[None, :], out_weight,
        expert_gate_up.reshape(-1, PAGE_TOKENS, expert_gate_up.shape[2]), expert_down[0],
    ))


def solution(mesh):
    return jax.shard_map(
        on_device,
        mesh=mesh,
        in_specs=(
            P(("parts", "ep"), None),
            P(("parts", "ep"), None),
            P(("parts", "ep"), None),
            P(("parts", "ep"), None, None),
            P(("parts", "ep"), None, None),
            P(("parts", "ep"), None),
            P(("parts", "ep"), None),
            P(("parts", "ep"), None),
            P("ep", None),
            P(),
            P(("parts", "ep"), None),
            P(("parts", "ep"), None),
            P("ep", None, None),
            P("ep", None, None),
            P(("parts", "ep"), None),
            P(("parts", "ep"), None),
        ),
        out_specs=(
            P(("parts", "ep"), None),
            P(("parts", "ep"), None, None),
            P(("parts", "ep"), None, None),
        ),
        check_vma=False,
    )
```

```python
import functools
import math

import jax
import jax.numpy as jnp
from jax import lax
from jax.experimental import pallas as pl
from jax.experimental.pallas import tpu as pltpu
from jax.sharding import PartitionSpec as P

QUERY_HEADS = 64
KEY_VALUE_HEADS = 4
HEAD_SIZE = 128
PAGE_TOKENS = 16
MOST_SEQ_PAGES = 16
SEQ_UNROLL = 4
PLANE = 4
MESH = pl.DeviceIdType.MESH


def layer_kernel(
    n, len_ref, order_ref, mig_page_ref, mig_dest_ref, ids_ref, weights_ref,
    q_hbm, fk_hbm, fv_hbm, k_hbm, v_hbm, hidden_hbm, gain_hbm, wo_hbm, wgu_hbm, wd_hbm,
    out_ref, ak_ref, av_ref,
    wo, wgu, wd, heads, gates, part, crecv, yrecv, zrecv, rows, act, mid, acc,
    q_in, qs, attn_ref, ks, vs, fresh, fkf, fvf, mk_ref, mv_ref, gate_ref, hidden_ref, gain_ref,
    wsem, asend, arecv, gsend, grecv, ksend, krecv, vsend, vrecv, rs, nsz, nsy, nsc, nrecv,
):
    G = n // PLANE
    me = lax.axis_index("ep")
    g = lax.div(me, PLANE)
    lane = lax.rem(me, PLANE)
    b = lax.div(lane, 2)
    c = lax.rem(lane, 2)
    S = hidden_ref.shape[0]
    D = hidden_ref.shape[1]
    FFW = wd_hbm.shape[0]
    block_rows = PLANE * S

    def dev(gg, bb, cc):
        return {"ep": gg * PLANE + bb * 2 + cc}

    def remote(src, dst, send, recv, to):
        return pltpu.make_async_remote_copy(
            src_ref=src, dst_ref=dst, send_sem=send, recv_sem=recv, device_id=to,
            device_id_type=MESH,
        )

    pages = k_hbm.shape[0]
    width = KEY_VALUE_HEADS * HEAD_SIZE
    kpool = wgu.at[0:pages, :, 0:width]
    vpool = wgu.at[0:pages, :, width:2 * width]
    load_k = pltpu.make_async_copy(k_hbm, kpool, wsem.at[0])
    load_v = pltpu.make_async_copy(v_hbm, vpool, wsem.at[1])
    load_q = pltpu.make_async_copy(q_hbm, q_in, wsem.at[2])
    load_fk = pltpu.make_async_copy(fk_hbm, fresh.at[0], wsem.at[3])
    load_fv = pltpu.make_async_copy(fv_hbm, fresh.at[1], wsem.at[4])
    load_wo = pltpu.make_async_copy(wo_hbm, wo, wsem.at[5])
    load_wd = pltpu.make_async_copy(wd_hbm, wd, wsem.at[6])
    load_hidden = pltpu.make_async_copy(hidden_hbm, hidden_ref, wsem.at[7])
    load_gain = pltpu.make_async_copy(gain_hbm, gain_ref, wsem.at[8])
    load_wgu = pltpu.make_async_copy(wgu_hbm, wgu, wsem.at[9])
    own_k = pltpu.make_async_copy(mk_ref.at[me], ak_ref.at[me], wsem.at[10])
    own_v = pltpu.make_async_copy(mv_ref.at[me], av_ref.at[me], wsem.at[11])
    for load in (load_q, load_fk, load_fv, load_k, load_v, load_wo, load_wd, load_hidden,
                 load_gain):
        load.start()

    barrier = pltpu.get_barrier_semaphore()

    @pl.loop(1, n)
    def _(i):
        pl.semaphore_signal(
            barrier, inc=1, device_id={"ep": lax.rem(me + i, n)}, device_id_type=MESH
        )

    experts = lax.broadcasted_iota(jnp.int32, (128, S), 0)
    table = jnp.zeros((128, S), jnp.float32)
    for k in range(ids_ref.shape[0]):
        table = table + jnp.where(experts == ids_ref[k:k + 1, :], weights_ref[k:k + 1, :], 0.0)
    table = jnp.concatenate([table, jnp.zeros((128, 128 - S), jnp.float32)], axis=1)
    for e in range(n):
        gate_ref[e] = jnp.broadcast_to(table[e:e + 1, :], (8, 128))
    gates[me] = gate_ref[me]

    def near(t):
        closest = jnp.minimum(g, G - 1 - g)
        away = lax.div(t + 1, 2)
        side = jnp.where(lax.rem(t, 2) == 1, g - away, g + away)
        rest = jnp.where(g + g <= G - 1, t, G - 1 - t)
        return jnp.where(t <= closest + closest, side, rest)

    def peer_of(k):
        plane = near(G - 1 - lax.div(k, PLANE))
        return plane * PLANE + lax.rem(lane + 1 + lax.rem(k, PLANE), PLANE)

    half_rows = S // 2

    def attn_copy(slot, peer, part_no):
        at = pl.ds(pl.multiple_of(part_no * half_rows, half_rows), half_rows)
        return remote(attn_ref.at[peer, at], heads.at[slot, at], asend.at[part_no, peer],
                      arecv.at[part_no, slot], {"ep": peer})

    def gate_copy(slot, peer):
        return remote(gate_ref.at[peer], gates.at[slot], gsend.at[peer], grecv.at[slot], {"ep": peer})

    def key_copy(slot, peer):
        return remote(mk_ref.at[peer], ak_ref.at[slot], ksend.at[peer], krecv.at[slot],
                      {"ep": peer})

    def value_copy(slot, peer):
        return remote(mv_ref.at[peer], av_ref.at[slot], vsend.at[peer], vrecv.at[slot],
                      {"ep": peer})

    def stage_pages(dest):
        page, found = jnp.int32(0), jnp.int32(0)
        for i in range(mig_page_ref.shape[1]):
            same = mig_dest_ref[0, i] == dest
            page = jnp.where(same, mig_page_ref[0, i], page)
            found = jnp.where(same, 1, found)
        keep = jnp.full((PAGE_TOKENS, width), found, jnp.int32) == 1
        zero = jnp.zeros((PAGE_TOKENS, width), jnp.float32)
        for pool, staged in ((0, mk_ref), (width, mv_ref)):
            rows_of = wgu[page, :, pool:pool + width].astype(jnp.float32)
            staged[dest] = jnp.where(keep, rows_of, zero).astype(jnp.bfloat16)

    load_q.wait()
    load_fk.wait()
    load_fv.wait()
    for h in range(QUERY_HEADS):
        qs[pl.ds(h, S, stride=QUERY_HEADS), :] = q_in[
            :, h * HEAD_SIZE:(h + 1) * HEAD_SIZE
        ].astype(jnp.float32)
    fkf[...] = fresh[0].astype(jnp.float32)
    fvf[...] = fresh[1].astype(jnp.float32)

    load_k.wait()
    load_v.wait()
    stage_pages(me)
    own_k.start()
    own_v.start()
    pl.semaphore_wait(barrier, n - 1)

    @pl.loop(0, n - 1)
    def _(k):
        peer = peer_of(k)
        stage_pages(peer)
        key_copy(me, peer).start()
        value_copy(me, peer).start()
        gate_copy(me, peer).start()

    group = QUERY_HEADS // KEY_VALUE_HEADS
    tokens = MOST_SEQ_PAGES * PAGE_TOKENS
    score_scale = 1.0 / math.sqrt(HEAD_SIZE)
    row_head = lax.broadcasted_iota(jnp.int32, (QUERY_HEADS, width), 0) // group
    col_head = lax.broadcasted_iota(jnp.int32, (QUERY_HEADS, width), 1) // HEAD_SIZE
    diagonal = (row_head == col_head).astype(jnp.float32).astype(jnp.bfloat16)
    place = lax.broadcasted_iota(jnp.int32, (QUERY_HEADS, tokens), 1)

    def attend_some(part_no, i, start):
        first = part_no * half_rows + i * SEQ_UNROLL
        several = range(SEQ_UNROLL)
        spans, lengths, q_wides, scores, owns, probs, own_probs, results = ([] for _ in range(8))
        for u in several:
            s = first + u
            lengths.append(len_ref[0, s])
            for p in range(MOST_SEQ_PAGES):
                page = order_ref[0, jnp.minimum(start + p, pages - 1)]
                ks[u, p * PAGE_TOKENS:(p + 1) * PAGE_TOKENS, :] = wgu[page, :, 0:width]
                vs[u, p * PAGE_TOKENS:(p + 1) * PAGE_TOKENS, :] = wgu[page, :, width:2 * width]
            start = start + lax.div(lengths[u] + (PAGE_TOKENS - 1), PAGE_TOKENS)
            spans.append(pl.ds(pl.multiple_of(s * QUERY_HEADS, QUERY_HEADS), QUERY_HEADS))
            q = qs[spans[u], :].astype(jnp.bfloat16)
            q_wides.append(jnp.concatenate([q] * KEY_VALUE_HEADS, axis=1) * diagonal)
        for u in several:
            scores.append(lax.dot_general(
                q_wides[u], ks[u], (((1,), (1,)), ((), ())), preferred_element_type=jnp.float32
            ) * score_scale)
        for u in several:
            owns.append(jnp.sum(
                q_wides[u].astype(jnp.float32) * fkf[pl.ds(first + u, 1), :], axis=1,
                keepdims=True,
            ) * score_scale)
        for u in several:
            masked = jnp.where(place < lengths[u], scores[u], -1e30)
            highest = jnp.maximum(jnp.max(masked, axis=1, keepdims=True), owns[u])
            weights = jnp.exp(masked - highest)
            own_weight = jnp.exp(owns[u] - highest)
            inverse = 1.0 / (jnp.sum(weights, axis=1, keepdims=True) + own_weight)
            probs.append((weights * inverse).astype(jnp.bfloat16))
            own_probs.append((own_weight * inverse).astype(jnp.bfloat16).astype(jnp.float32))
        for u in several:
            mixed = jnp.dot(probs[u], vs[u], preferred_element_type=jnp.float32)
            fresh_value = fvf[pl.ds(first + u, 1), :]
            results.append(jnp.concatenate(
                [
                    mixed[h * group:(h + 1) * group, h * HEAD_SIZE:(h + 1) * HEAD_SIZE]
                    + own_probs[u][h * group:(h + 1) * group]
                    * fresh_value[:, h * HEAD_SIZE:(h + 1) * HEAD_SIZE]
                    for h in range(KEY_VALUE_HEADS)
                ],
                axis=0,
            ))
        for u in several:
            qs[spans[u], :] = results[u]
        return start

    some = half_rows // SEQ_UNROLL
    head_share = QUERY_HEADS // n

    def attend_half(part_no, start):
        start = lax.fori_loop(0, some, functools.partial(attend_some, part_no), start)
        at = pl.ds(pl.multiple_of(part_no * half_rows, half_rows), half_rows)
        first = part_no * (half_rows * QUERY_HEADS)
        for h in range(QUERY_HEADS):
            d, j = h // head_share, h % head_share
            attn_ref[d, at, j * HEAD_SIZE:(j + 1) * HEAD_SIZE] = qs[
                pl.ds(first + h, half_rows, stride=QUERY_HEADS), :
            ].astype(jnp.bfloat16)

        @pl.loop(0, n - 1)
        def _(k):
            attn_copy(me, peer_of(k), part_no).start()

        return start

    lax.fori_loop(0, 2, attend_half, jnp.int32(0))
    heads[me] = attn_ref[me]
    load_wgu.start()

    def c_copy(r, gi):
        return remote(part.at[gi, :, 1 - c], crecv.at[r, gi], rs.at[r, 0, gi], rs.at[r, 1, gi],
                      dev(g, b, 1 - c))

    def y_copy(r, gi):
        return remote(crecv.at[r, gi, 1 - b], yrecv.at[r, gi], rs.at[r, 2, gi], rs.at[r, 3, gi],
                      dev(g, 1 - b, c))

    def z_copy(r, gi, slot):
        return remote(yrecv.at[r, gi], zrecv.at[r, slot], rs.at[r, 4, gi], rs.at[r, 5, slot],
                      dev(gi, b, c))

    def core_stage(r, gi):
        c_copy(r, gi).wait_recv()
        for bb in range(2):
            crecv[r, gi, bb] = (
                part[gi, bb, c].astype(jnp.float32) + crecv[r, gi, bb].astype(jnp.float32)
            ).astype(jnp.bfloat16)
        y_copy(r, gi).start()

    def y_stage(r, gi):
        y_copy(r, gi).wait_recv()
        yrecv[r, gi] = (
            crecv[r, gi, b].astype(jnp.float32) + yrecv[r, gi].astype(jnp.float32)
        ).astype(jnp.bfloat16)

    def line_copy(gi):
        step = jnp.where(gi > g, 1, -1)
        slot = jnp.where((step < 0) & (g + step == gi), G, gi)
        return remote(yrecv.at[0, gi], zrecv.at[0, slot], rs.at[0, 4, gi], rs.at[0, 5, slot],
                      dev(g + step, b, c))

    def line_arrival(slot):
        return remote(zrecv.at[0, slot], zrecv.at[0, slot], rs.at[0, 4, 0], rs.at[0, 5, slot],
                      dev(g, b, 1 - c))

    def starts_line(gi):
        return ((gi > g) & (g == 0)) | ((gi < g) & (g == G - 1))

    def line_stage(gi):
        line_arrival(gi).wait_recv()
        yrecv[0, gi] = (
            yrecv[0, gi].astype(jnp.float32) + zrecv[0, gi].astype(jnp.float32)
        ).astype(jnp.bfloat16)
        line_copy(gi).start()

    def collect_line():
        acc[...] = yrecv[0, g].astype(jnp.float32)
        for slot, there in ((g, g > 0), (G, g < G - 1)):
            @pl.when(there)
            def _():
                line_arrival(slot).wait_recv()
                acc[...] += zrecv[0, slot].astype(jnp.float32)

    def collect(r):
        acc[...] = yrecv[r, g].astype(jnp.float32)

        @pl.loop(1, G)
        def _(i):
            src = lax.rem(g + i, G)
            z_copy(r, g, src).wait_recv()
            acc[...] += zrecv[r, src].astype(jnp.float32)

    load_wo.wait()
    tile = 1024

    @pl.loop(0, G + 2)
    def _(t):
        @pl.when(t < G)
        def _():
            gi = near(G - 1 - t)
            for j in range(PLANE):
                src = gi * PLANE + j

                @pl.when(src != me)
                def _():
                    attn_copy(src, src, 0).wait_recv()
                    attn_copy(src, src, 1).wait_recv()

            left = heads[pl.ds(gi * PLANE, PLANE)].reshape(block_rows, heads.shape[2])
            for j in range(D // tile):
                part[gi, :, :, :, j * tile:(j + 1) * tile] = jnp.dot(
                    left, wo[:, j * tile:(j + 1) * tile], preferred_element_type=jnp.float32
                ).astype(jnp.bfloat16).reshape(2, 2, S, tile)
            c_copy(0, gi).start()

        @pl.when((t >= 1) & (t <= G))
        def _():
            core_stage(0, near(G - t))

        @pl.when(t >= 3)
        def _():
            gi = near(G + 2 - t)

            @pl.when(jnp.logical_not(starts_line(gi)))
            def _():
                line_stage(gi)

        @pl.when(t >= 2)
        def _():
            gi = near(G + 1 - t)
            y_stage(0, gi)

            @pl.when(starts_line(gi))
            def _():
                line_copy(gi).start()

    collect_line()
    load_hidden.wait()
    load_gain.wait()
    middle = (hidden_ref[...].astype(jnp.float32) + acc[...]).astype(jnp.bfloat16)
    mid[...] = middle
    middle = middle.astype(jnp.float32)
    scale = lax.rsqrt(jnp.mean(middle * middle, axis=1, keepdims=True) + 1e-06)
    rows[g, b, c] = (middle * scale * gain_ref[...]).astype(jnp.bfloat16)

    def row_copy(gg, bb, cc, send, to):
        slot = rows.at[gg, bb, cc]
        return remote(slot, slot, send, nrecv.at[gg, bb, cc], to)

    def rows_to_z(gg, step):
        return row_copy(gg, b, c, nsz.at[gg, (step + 1) // 2], dev(g + step, b, c))

    def pass_on(gg, act_on):
        @pl.when((gg <= g) & (g + 1 < G))
        def _():
            act_on(rows_to_z(gg, 1))

        @pl.when((gg >= g) & (g >= 1))
        def _():
            act_on(rows_to_z(gg, -1))

    def rows_to_y(gg):
        return row_copy(gg, b, c, nsy.at[gg], dev(g, 1 - b, c))

    def rows_to_core(gg, bb):
        return row_copy(gg, bb, c, nsc.at[gg, bb], dev(g, b, 1 - c))

    def arrival(gg, bb, cc):
        return row_copy(gg, bb, cc, nsy.at[gg], dev(g, b, 1 - c))

    rows_to_core(g, b).start()
    rows_to_y(g).start()

    pass_on(g, lambda copy: copy.start())

    @pl.loop(0, n - 1)
    def _(k):
        peer = peer_of(k)
        gate_copy(peer, peer).wait_recv()

    @pl.loop(0, G)
    def _(gi):
        c_copy(0, gi).wait_send()

    load_wgu.wait()
    load_wd.wait()
    half = 256

    def take_along_z(gi):
        arrival(gi, b, c).wait_recv()
        pass_on(gi, lambda copy: copy.start())
        rows_to_y(gi).start()
        rows_to_core(gi, b).start()

    def turn(t):
        return near(lax.rem(t + 1, G))

    @pl.loop(0, G + 2)
    def _(t):
        @pl.when((t == 0) & (G > 1))
        def _():
            take_along_z(near(1))

        @pl.when(t + 2 < G)
        def _():
            take_along_z(near(t + 2))

        @pl.when(t < G)
        def _():
            gi = turn(t)
            arrival(gi, 1 - b, c).wait_recv()
            rows_to_core(gi, 1 - b).start()
            arrival(gi, b, 1 - c).wait_recv()
            arrival(gi, 1 - b, 1 - c).wait_recv()

            @pl.loop(0, FFW // half)
            def _(j):
                left = rows[gi].reshape(block_rows, D)
                at = pl.multiple_of(j * half, half)
                gate = jnp.dot(left, wgu[:, :, pl.ds(at, half)].reshape(D, half),
                               preferred_element_type=jnp.float32)
                up = jnp.dot(left, wgu[:, :, pl.ds(FFW + at, half)].reshape(D, half),
                             preferred_element_type=jnp.float32)
                act[:, pl.ds(at, half)] = (gate * jax.nn.sigmoid(gate) * up).astype(jnp.bfloat16)

            tiles = gates[pl.ds(gi * PLANE, PLANE)]
            token = lax.broadcasted_iota(jnp.int32, (S, 128), 0)
            same = token == lax.broadcasted_iota(jnp.int32, (S, 128), 1)
            chosen = jnp.concatenate(
                [
                    jnp.sum(
                        jnp.where(same, jnp.broadcast_to(tiles[j, 0:1, :], (S, 128)), 0.0),
                        axis=1, keepdims=True,
                    )
                    for j in range(PLANE)
                ],
                axis=0,
            )
            for j in range(D // tile):
                y = jnp.dot(act[...], wd[:, j * tile:(j + 1) * tile],
                            preferred_element_type=jnp.float32)
                y = y.astype(jnp.bfloat16).astype(jnp.float32) * chosen
                part[gi, :, :, :, j * tile:(j + 1) * tile] = y.astype(jnp.bfloat16).reshape(
                    2, 2, S, tile
                )
            c_copy(1, gi).start()

        @pl.when((t >= 1) & (t <= G))
        def _():
            core_stage(1, turn(t - 1))

        @pl.when(t >= 2)
        def _():
            gi = turn(t - 2)
            y_stage(1, gi)

            @pl.when(t <= G)
            def _():
                z_copy(1, gi, g).start()

    collect(1)
    out_ref[...] = (mid[...].astype(jnp.float32) + acc[...]).astype(jnp.bfloat16)

    own_k.wait()
    own_v.wait()

    @pl.loop(0, n - 1)
    def _(k):
        peer = peer_of(k)
        attn_copy(me, peer, 0).wait_send()
        attn_copy(me, peer, 1).wait_send()
        gate_copy(me, peer).wait_send()
        key_copy(me, peer).wait_send()
        value_copy(me, peer).wait_send()
        key_copy(peer, peer).wait_recv()
        value_copy(peer, peer).wait_recv()

    @pl.loop(0, G)
    def _(gi):
        c_copy(1, gi).wait_send()
        rows_to_y(gi).wait_send()
        rows_to_core(gi, 0).wait_send()
        rows_to_core(gi, 1).wait_send()
        pass_on(gi, lambda copy: copy.wait_send())
        for r in range(2):
            y_copy(r, gi).wait_send()

    @pl.loop(1, G)
    def _(i):
        gi = lax.rem(g + i, G)
        line_copy(gi).wait_send()
        z_copy(1, gi, g).wait_send()


def layer(n, lengths, page_order, mig_pages, mig_dest, ids, weights, queries, fresh_keys,
          fresh_values, keys, values, hidden, gain, wo, wgu, wd):
    G = n // PLANE
    S, D = hidden.shape
    FFW = wd.shape[0]
    width = KEY_VALUE_HEADS * HEAD_SIZE
    tokens = MOST_SEQ_PAGES * PAGE_TOKENS
    pages = (n, PAGE_TOKENS, width)
    smem = pl.BlockSpec(memory_space=pltpu.SMEM)
    vmem = pl.BlockSpec(memory_space=pltpu.VMEM)
    anywhere = pl.BlockSpec(memory_space=pl.ANY)
    bf16 = jnp.bfloat16
    dma = pltpu.SemaphoreType.DMA
    return pl.pallas_call(
        functools.partial(layer_kernel, n),
        out_shape=(
            jax.ShapeDtypeStruct(hidden.shape, bf16),
            jax.ShapeDtypeStruct(pages, bf16),
            jax.ShapeDtypeStruct(pages, bf16),
        ),
        in_specs=[smem] * 4 + [vmem] * 2 + [anywhere] * 10,
        out_specs=(vmem, anywhere, anywhere),
        scratch_shapes=[
            pltpu.VMEM(wo.shape, bf16),
            pltpu.VMEM(wgu.shape, bf16),
            pltpu.VMEM(wd.shape, bf16),
            pltpu.VMEM((n, S, wo.shape[0]), bf16),
            pltpu.VMEM((n, 8, 128), jnp.float32),
            pltpu.VMEM((G, 2, 2, S, D), bf16),
            pltpu.VMEM((2, G, 2, S, D), bf16),
            pltpu.VMEM((2, G, S, D), bf16),
            pltpu.VMEM((2, G + 1, S, D), bf16),
            pltpu.VMEM((G, 2, 2, S, D), bf16),
            pltpu.VMEM((PLANE * S, FFW), bf16),
            pltpu.VMEM((S, D), bf16),
            pltpu.VMEM((S, D), jnp.float32),
            pltpu.VMEM(queries.shape, bf16),
            pltpu.VMEM((S * QUERY_HEADS, HEAD_SIZE), jnp.float32),
            pltpu.VMEM((n, S, wo.shape[0]), bf16),
            pltpu.VMEM((SEQ_UNROLL, tokens, width), bf16),
            pltpu.VMEM((SEQ_UNROLL, tokens, width), bf16),
            pltpu.VMEM((2, S, width), bf16),
            pltpu.VMEM((S, width), jnp.float32),
            pltpu.VMEM((S, width), jnp.float32),
            pltpu.VMEM(pages, bf16),
            pltpu.VMEM(pages, bf16),
            pltpu.VMEM((n, 8, 128), jnp.float32),
            pltpu.VMEM(hidden.shape, bf16),
            pltpu.VMEM(gain.shape, jnp.float32),
            dma((12,)),
            dma((2, n)), dma((2, n)), dma((n,)), dma((n,)),
            dma((n,)), dma((n,)), dma((n,)), dma((n,)),
            dma((2, 6, G + 1)),
            dma((G, 2)), dma((G,)), dma((G, 2)), dma((G, 2, 2)),
        ],
        compiler_params=pltpu.CompilerParams(
            collective_id=0, has_side_effects=True, vmem_limit_bytes=63 * 1024 * 1024
        ),
    )(lengths, page_order, mig_pages, mig_dest, ids, weights, queries, fresh_keys, fresh_values,
      keys, values, hidden, gain, wo, wgu, wd)


def hand_out_kernel(a_ref, b_ref, c_ref, x_ref, y_ref, z_ref, a_held, b_held, c_held, sem):
    moves = (
        (a_ref, a_held, x_ref), (b_ref, b_held, y_ref), (c_ref, c_held, z_ref)
    )
    loads = [pltpu.make_async_copy(s, h, sem.at[0, i]) for i, (s, h, _) in enumerate(moves)]
    stores = [pltpu.make_async_copy(h, t, sem.at[1, i]) for i, (_, h, t) in enumerate(moves)]
    for load in loads:
        load.start()
    for load, store in zip(loads, stores):
        load.wait()
        store.start()
    for store in stores:
        store.wait()


def hand_out(*results):
    anywhere = pl.BlockSpec(memory_space=pl.ANY)
    return pl.pallas_call(
        hand_out_kernel,
        out_shape=tuple(jax.ShapeDtypeStruct(r.shape, r.dtype) for r in results),
        in_specs=[anywhere] * 3,
        out_specs=(anywhere,) * 3,
        scratch_shapes=[pltpu.VMEM(r.shape, r.dtype) for r in results]
        + [pltpu.SemaphoreType.DMA((2, 3))],
    )(*results)


def on_device(
    queries, fresh_token_keys, fresh_token_values, pooled_keys, pooled_values, lengths, page_order,
    hidden, out_weight, norm_gain, expert_ids, gate_weights, expert_gate_up, expert_down,
    mig_pages, mig_dest,
):
    n = lax.axis_size("ep")
    return hand_out(*layer(
        n, lengths, page_order, mig_pages, mig_dest.T, expert_ids.T, gate_weights.T, queries,
        fresh_token_keys, fresh_token_values, pooled_keys,
        pooled_values, hidden, norm_gain[None, :], out_weight,
        expert_gate_up.reshape(-1, PAGE_TOKENS, expert_gate_up.shape[2]), expert_down[0],
    ))


def solution(mesh):
    return jax.shard_map(
        on_device,
        mesh=mesh,
        in_specs=(
            P(("parts", "ep"), None),
            P(("parts", "ep"), None),
            P(("parts", "ep"), None),
            P(("parts", "ep"), None, None),
            P(("parts", "ep"), None, None),
            P(("parts", "ep"), None),
            P(("parts", "ep"), None),
            P(("parts", "ep"), None),
            P("ep", None),
            P(),
            P(("parts", "ep"), None),
            P(("parts", "ep"), None),
            P("ep", None, None),
            P("ep", None, None),
            P(("parts", "ep"), None),
            P(("parts", "ep"), None),
        ),
        out_specs=(
            P(("parts", "ep"), None),
            P(("parts", "ep"), None, None),
            P(("parts", "ep"), None, None),
        ),
        check_vma=False,
    )
```
